512 devices in a mesh: dp: 128 (over y, z, core), tensor: 4 (over x).
Axes of the slice: x: 4, y: 4, z: 16, core: 2. Of those that a mesh axis runs over, the one named last changes fastest.
Arguments:
- tokens: bfloat16 [32768, 4096], P('dp', 'tensor'), may hold values from -6 to 6
- out_grad: bfloat16 [32768, 14336], P('dp', 'tensor'), may hold values from -6 to 6
- proj_in: bfloat16 [4096, 64], P('tensor'), may hold values from -0.09375 to 0.09375
- proj_out: bfloat16 [14336, 64], P('tensor'), may hold values from -0.046875 to 0.046875
- source_ids: int32 [512], P('dp'), may hold values from 0 to 255, as said below
- slot_of_source: int32 [256], replicated, may hold values from 0 to 255, as said below
Outputs:
- source_sketch: float32 [256, 4096], P('dp', 'tensor')
The draws below stay inside these ranges and needn't reach their ends.
Inputs may be any that keep to these rules, and one draw needn't show every extreme that they name: `source_ids`: sequences j * 4, j * 4 + 1 and j * 4 + 2 belong to sources whose output rows lie in the blocks of 2 rows numbered j - 1, j + 1 and j + 64, counted round; the other sequences' sources follow a skewed law. `slot_of_source`: each output row is named by exactly one source.
All inputs are finite; a program needn't handle non-finite values.
Results may differ from the reference program's by a relative error of at most 0.0003.
Values sent between devices are 32-bit elements; how exact they have to be, the bound alone decides.
A program may use at most 64 MiB of HBM per device.

```python
import jax
import jax.numpy as jnp
from jax import lax

D = 4096
FF = 14336
R = 64
LEN = 64
SEQ_DEV = 4
SRC_DEV = 2
TOKENS = 32768
SEQS = 512
SOURCES = 256


def shared_order(key):
    return jax.random.permutation(jax.random.fold_in(key, 11), SOURCES).astype(jnp.int32)


def draw_slot_of_source(key, part):
    order = shared_order(key)
    return order.astype(jnp.int32)


def draw_source_ids(key, part):
    order = shared_order(key)
    key = jax.random.fold_in(key, 5)
    owners = SOURCES // SRC_DEV
    source_at_slot = jnp.argsort(order, stable=True).astype(jnp.int32)
    index = jnp.arange(SEQS, dtype=jnp.int32)
    device = index // SEQ_DEV
    position = index % SEQ_DEV
    offset = jnp.where(position == 0, owners - 1, jnp.where(position == 1, 1, owners // 2)).astype(jnp.int32)
    target = (device + offset) % owners
    within = jax.random.randint(jax.random.fold_in(key, 1), (SEQS,), 0, SRC_DEV).astype(jnp.int32)
    forced = source_at_slot[target * SRC_DEV + within]
    ranks = jnp.arange(SOURCES, dtype=jnp.int32)
    weights = (65536 // (ranks + 1)).astype(jnp.int32)
    bounds = jnp.cumsum(weights).astype(jnp.int32)
    picks = jax.random.randint(jax.random.fold_in(key, 2), (SEQS,), 0, bounds[-1]).astype(jnp.int32)
    rank = jnp.sum((picks[:, None] >= bounds[None, :]).astype(jnp.int32), axis=1).astype(jnp.int32)
    rank_map = jax.random.permutation(jax.random.fold_in(key, 3), SOURCES).astype(jnp.int32)
    skewed = rank_map[rank]
    return jnp.where(position < 3, forced, skewed).astype(jnp.int32)


def steps_of(key, extent, pieces, low, high):
    factor_of, own = 1.0, jax.random.fold_in(key, 6)
    for axis_at, blocks in pieces:
        heights = jnp.exp(jax.random.uniform(jax.random.fold_in(own, axis_at), (blocks,), jnp.float32, low / len(pieces), high / len(pieces)))
        factor_of = factor_of * jnp.repeat(heights, extent[axis_at] // blocks).reshape([-1 if axis == axis_at else 1 for axis in range(len(extent))])
    return factor_of


def centred(stream_key, extent, scale, most, split=(), held_as=jnp.bfloat16):
    values = scale * jax.random.normal(stream_key, extent, jnp.float32)
    if split:
        values = values * steps_of(stream_key, extent, split, -0.22, 0.18)
    return jnp.clip(values, -most, most).astype(held_as)


def setup_inputs(seed: int = 0) -> dict:
    keys = jax.random.split(jax.random.key(seed), 7)
    return {
        "tokens": centred(keys[0], (TOKENS, D), 1.0, 6.0, ((0, 128), (1, 4))),
        "out_grad": centred(keys[1], (TOKENS, FF), 1.0, 6.0, ((0, 128), (1, 4))),
        "proj_in": centred(keys[2], (D, R), D ** -0.5, 0.09375, ((0, 4),)),
        "proj_out": centred(keys[3], (FF, R), FF ** -0.5, 0.046875, ((0, 4),)),
        "source_ids": draw_source_ids(jax.random.fold_in(keys[6], 71), 0),
        "slot_of_source": draw_slot_of_source(jax.random.fold_in(keys[6], 71), 0),
    }


def reference(tokens, out_grad, proj_in, proj_out, source_ids, slot_of_source):
    xp = jnp.dot(tokens, proj_in, preferred_element_type=jnp.float32)
    gp = jnp.dot(out_grad, proj_out, preferred_element_type=jnp.float32)
    xs = xp.reshape(SEQS, LEN, R)
    gs = gp.reshape(SEQS, LEN, R)
    sketch = jnp.einsum("sla,slb->sab", gs, xs, precision=lax.Precision.HIGHEST) * (LEN ** -0.5)
    slots = slot_of_source[source_ids].astype(jnp.int32)
    summed = jax.ops.segment_sum(sketch.reshape(SEQS, R * R), slots, num_segments=SOURCES)
    return summed
```

```python
import functools

import jax
import jax.numpy as jnp
from jax import lax
from jax.experimental import pallas as pl
from jax.experimental.pallas import tpu as pltpu
from jax.sharding import PartitionSpec as P

MESH = pl.DeviceIdType.MESH
F32 = jnp.float32
CORES = 2
COLUMNS = 4


def project(rows, weights):
    return lax.dot_general(rows, weights, (((1,), (1,)), ((), ())), preferred_element_type=F32)


def kernel(
    ny, nz, nx, length,
    tok_hbm, og_hbm, pin_hbm, pout_hbm, src_hbm, slot_hbm,
    out_ref,
    tok, og, pin, pout, src, slot_of,
    mine_last, mine_rest, recv_last, recv_rest, gram,
    held, ids, fixed_out, fixed_in, spread_out, spread_in,
    load_sem, xl_send, xl_recv, xr_send, xr_recv,
    id_send, id_recv, gather_send, gather_recv,
    fixed_send, fixed_recv, spread_send, spread_recv,
):
    j = lax.axis_index("dp")
    m = lax.axis_index("tensor")
    ndp = ny * nz * CORES
    half = ndp // 2
    core = lax.rem(j, CORES)
    z = lax.rem(lax.div(j, CORES), nz)
    y = lax.div(j, CORES * nz)
    rest = 3 * length
    quarter = 64 // nx

    def dp_of(yy, zz, cc):
        return (yy * nz + zz) * CORES + cc

    loads = [
        (src_hbm, src),
        (slot_hbm, slot_of),
        (pout_hbm, pout),
        (og_hbm.at[pl.ds(rest, length)], og.at[pl.ds(rest, length)]),
        (pin_hbm, pin),
        (tok_hbm.at[pl.ds(rest, length)], tok.at[pl.ds(rest, length)]),
        (og_hbm.at[pl.ds(0, rest)], og.at[pl.ds(0, rest)]),
        (tok_hbm.at[pl.ds(0, rest)], tok.at[pl.ds(0, rest)]),
    ]
    loads = [pltpu.make_async_copy(a, b, load_sem.at[i]) for i, (a, b) in enumerate(loads)]
    for load in loads:
        load.start()

    barrier = pltpu.get_barrier_semaphore()
    x_peers = [(j, lax.rem(m + d, nx)) for d in range(1, nx)]
    z_peers = [(dp_of(y, lax.rem(z + d, nz), core), m) for d in range(1, nz)]
    spread = [(dy, dc) for dy in range(ny) for dc in range(CORES)]
    spread_peers = [
        (dp_of(lax.rem(y + dy, ny), z, lax.rem(core + dc, CORES)), m) for dy, dc in spread
    ]
    fixed_to = [lax.rem(j + ndp - 1, ndp), lax.rem(j + 1, ndp), lax.rem(j + half, ndp)]
    fixed_peers = [(t, m) for t in fixed_to]
    greeted = x_peers + z_peers + spread_peers[1:] + fixed_peers
    for peer in greeted:
        pl.semaphore_signal(barrier, inc=1, device_id=peer, device_id_type=MESH)

    loads[0].wait()
    loads[1].wait()
    slots = [slot_of[src[i]] for i in range(4)]
    ids[0] = jnp.full((1, 128), slots[3], jnp.int32)

    for i in (2, 3, 4, 5):
        loads[i].wait()
    xp = project(tok[pl.ds(rest, length), :], pin[...])
    gp = project(og[pl.ds(rest, length), :], pout[...])
    mine_last[...] = jnp.concatenate([xp, gp], axis=1)

    pl.semaphore_wait(barrier, len(greeted))
    for d in range(1, nx):
        pltpu.make_async_remote_copy(
            mine_last, recv_last.at[nx - 1 - d], xl_send, xl_recv,
            device_id=x_peers[d - 1], device_id_type=MESH,
        ).start()
    for d in range(1, nz):
        pltpu.make_async_remote_copy(
            ids.at[0], ids.at[nz - d], id_send, id_recv,
            device_id=z_peers[d - 1], device_id_type=MESH,
        ).start()

    loads[6].wait()
    loads[7].wait()
    xp = project(tok[pl.ds(0, rest), :], pin[...])
    gp = project(og[pl.ds(0, rest), :], pout[...])
    mine_rest[...] = jnp.concatenate([xp, gp], axis=1)
    for d in range(1, nx):
        pltpu.make_async_remote_copy(
            mine_rest, recv_rest.at[nx - 1 - d], xr_send, xr_recv,
            device_id=x_peers[d - 1], device_id_type=MESH,
        ).start()

    lane = lax.broadcasted_iota(jnp.int32, (8, 128), 1)

    def sketch(total, at):
        gram[at] = lax.dot_general(
            total, total, (((0,), (0,)), ((), ())),
            precision=lax.Precision.HIGHEST, preferred_element_type=F32,
        ) * (length ** -0.5)
        start = 64 + m * quarter
        even = gram[at, pl.ds(start, quarter // 2, stride=2), :]
        odd = gram[at, pl.ds(start + 1, quarter // 2, stride=2), :]
        return jnp.where(lane < 64, even, pltpu.roll(odd, 64, 1))

    pltpu.make_async_copy(recv_last, recv_last, xl_recv).wait()
    total = mine_last[...]
    for d in range(nx - 1):
        total = total + recv_last[d]
    held[0] = sketch(total, 0)
    for d in range(1, nz):
        pltpu.make_async_remote_copy(
            held.at[0], held.at[nz - d], gather_send, gather_recv,
            device_id=z_peers[d - 1], device_id_type=MESH,
        ).start()

    pltpu.make_async_copy(recv_rest, recv_rest, xr_recv).wait()
    for s in range(3):
        rows = pl.ds(s * length, length)
        total = mine_rest[rows, :]
        for d in range(nx - 1):
            total = total + recv_rest[d, rows, :]
        value = sketch(total, 1 + s)
        for w in range(2):
            weight = jnp.where(slots[s] == fixed_to[s] * 2 + w, 1.0, 0.0).astype(F32)
            fixed_out[s, w] = value * weight
        pltpu.make_async_remote_copy(
            fixed_out.at[s], fixed_in.at[s], fixed_send.at[s], fixed_recv.at[s],
            device_id=fixed_peers[s], device_id_type=MESH,
        ).start()

    pltpu.make_async_copy(ids.at[pl.ds(1, nz - 1)], ids.at[pl.ds(1, nz - 1)], id_recv).wait()
    pltpu.make_async_copy(held.at[pl.ds(1, nz - 1)], held.at[pl.ds(1, nz - 1)], gather_recv).wait()
    for t in list(range(1, len(spread))) + [0]:
        dy, dc = spread[t]
        base = spread_peers[t][0] * 2
        for w in range(2):
            acc = jnp.zeros((8, 128), F32)
            for i in range(nz):
                acc = acc + jnp.where(ids[i] == base + w, held[i], 0.0)
            spread_out[t, w] = acc
        if t:
            back = ((ny - dy) % ny) * CORES + dc
            pltpu.make_async_remote_copy(
                spread_out.at[t], spread_in.at[back], spread_send, spread_recv,
                device_id=spread_peers[t], device_id_type=MESH,
            ).start()

    for s in range(3):
        pltpu.make_async_copy(fixed_in.at[s], fixed_in.at[s], fixed_recv.at[s]).wait()
    landed = spread_in.at[pl.ds(1, len(spread) - 1)]
    pltpu.make_async_copy(landed, landed, spread_recv).wait()
    for w in range(2):
        acc = spread_out[0, w]
        for s in range(3):
            acc = acc + fixed_in[s, w]
        for t in range(1, len(spread)):
            acc = acc + spread_in[t, w]
        out_ref[w] = acc

    pltpu.make_async_copy(recv_last, recv_last, xl_send).wait()
    pltpu.make_async_copy(recv_rest, recv_rest, xr_send).wait()
    pltpu.make_async_copy(ids.at[pl.ds(1, nz - 1)], ids.at[pl.ds(1, nz - 1)], id_send).wait()
    pltpu.make_async_copy(held.at[pl.ds(1, nz - 1)], held.at[pl.ds(1, nz - 1)], gather_send).wait()
    for s in range(3):
        pltpu.make_async_copy(fixed_out.at[s], fixed_out.at[s], fixed_send.at[s]).wait()
    pltpu.make_async_copy(landed, landed, spread_send).wait()


def local(ny, nz, nx, tokens, out_grad, proj_in, proj_out, source_ids, slot_of_source):
    length = tokens.shape[0] // source_ids.shape[0]
    width = 2 * proj_in.shape[1]
    pin, pout = proj_in.T, proj_out.T
    spread = ny * CORES
    dma = pltpu.SemaphoreType.DMA
    out = pl.pallas_call(
        functools.partial(kernel, ny, nz, nx, length),
        out_shape=jax.ShapeDtypeStruct((2, 8, 128), F32),
        in_specs=[pl.BlockSpec(memory_space=pltpu.HBM)] * 6,
        out_specs=pl.BlockSpec(memory_space=pltpu.VMEM),
        scratch_shapes=[
            pltpu.VMEM(tokens.shape, tokens.dtype),
            pltpu.VMEM(out_grad.shape, out_grad.dtype),
            pltpu.VMEM(pin.shape, pin.dtype),
            pltpu.VMEM(pout.shape, pout.dtype),
            pltpu.SMEM(source_ids.shape, jnp.int32),
            pltpu.SMEM(slot_of_source.shape, jnp.int32),
            pltpu.VMEM((length, width), F32),
            pltpu.VMEM((3 * length, width), F32),
            pltpu.VMEM((nx - 1, length, width), F32),
            pltpu.VMEM((nx - 1, 3 * length, width), F32),
            pltpu.VMEM((4, width, width), F32),
            pltpu.VMEM((nz, 8, 128), F32),
            pltpu.VMEM((nz, 1, 128), jnp.int32),
            pltpu.VMEM((3, 2, 8, 128), F32),
            pltpu.VMEM((3, 2, 8, 128), F32),
            pltpu.VMEM((spread, 2, 8, 128), F32),
            pltpu.VMEM((spread, 2, 8, 128), F32),
            dma((8,)), dma, dma, dma, dma, dma, dma, dma, dma, dma((3,)), dma((3,)), dma, dma,
        ],
        compiler_params=pltpu.CompilerParams(
            collective_id=0, has_side_effects=True, vmem_limit_bytes=60 * 2**20
        ),
    )(tokens, out_grad, pin, pout, source_ids, slot_of_source)
    return out.reshape(2, 8 * 128)


def solution(mesh):
    nx, ndp = mesh.shape["tensor"], mesh.shape["dp"]
    ny = COLUMNS
    nz = ndp // (ny * CORES)
    placed = (
        P("dp", "tensor"),
        P("dp", "tensor"),
        P("tensor", None),
        P("tensor", None),
        P("dp"),
        P(),
    )
    return jax.shard_map(
        functools.partial(local, ny, nz, nx),
        mesh=mesh, in_specs=placed, out_specs=P("dp", "tensor"), check_vma=False,
    )
```

```python
import functools

import jax
import jax.numpy as jnp
from jax import lax
from jax.experimental import pallas as pl
from jax.experimental.pallas import tpu as pltpu
from jax.sharding import PartitionSpec as P

MESH = pl.DeviceIdType.MESH
F32 = jnp.float32
CORES = 2
COLUMNS = 4
PACKED = 40


def product(a, b):
    return lax.dot_general(a, b, (((1,), (1,)), ((), ())), preferred_element_type=F32)


def kernel(
    ny, nz, nx, length,
    tok_hbm, og_hbm, pin_hbm, pout_hbm, src_hbm, slot_hbm,
    out_ref,
    tok, og, pin, pout, src, slot_of, gpt,
    mine_last, mine_rest, recv_last, recv_rest,
    held, ids, fixed_out, fixed_in, z_out, z_in,
    load_sem, xl_send, xl_recv, xr_send, xr_recv,
    id_send, id_recv, held_send, held_recv,
    fixed_send, fixed_recv, z_send, z_recv, token_a, token_b,
):
    j = lax.axis_index("dp")
    m = lax.axis_index("tensor")
    ndp = ny * nz * CORES
    half = ndp // 2
    core = lax.rem(j, CORES)
    z = lax.rem(lax.div(j, CORES), nz)
    y = lax.div(j, CORES * nz)

    def dp_of(yy, zz, cc):
        return (yy * nz + zz) * CORES + cc

    def rows_of(s):
        return pl.ds(s * length, length)

    last, rest = rows_of(3), pl.ds(0, 3 * length)
    loads = [
        (pout_hbm, pout),
        (og_hbm.at[last], og.at[last]),
        (pin_hbm, pin),
        (tok_hbm.at[last], tok.at[last]),
        (src_hbm, src),
        (slot_hbm, slot_of),
        (og_hbm.at[rest], og.at[rest]),
        (tok_hbm.at[rest], tok.at[rest]),
    ]
    loads = [pltpu.make_async_copy(a, b, load_sem.at[i]) for i, (a, b) in enumerate(loads)]
    for load in loads:
        load.start()

    def z_peers(offsets):
        offsets = sorted({d % nz for d in offsets} - {0})
        return [(dp_of(y, lax.rem(z + d, nz), core), m) for d in offsets]

    def greet(sem, peers):
        for peer in peers:
            pl.semaphore_signal(sem, inc=1, device_id=peer, device_id_type=MESH)

    x_peers = [(j, lax.rem(m + d, nx)) for d in range(1, nx)]
    spread = [(dy, dc) for dy in range(ny) for dc in range(CORES)]
    spread_peers = [
        (dp_of(lax.rem(y + dy, ny), z, lax.rem(core + dc, CORES)), m) for dy, dc in spread
    ]
    fixed_to = [lax.rem(j + ndp - 1, ndp), lax.rem(j + 1, ndp), lax.rem(j + half, ndp)]
    beside = lax.rem(j + ndp + 2 * core - 1, ndp)
    near = x_peers + spread_peers[1:] + z_peers((1, 2, -1, -2)) + [(beside, m)]
    two_off, four_off = z_peers((2, -2)), z_peers((4, -4))
    barrier = pltpu.get_barrier_semaphore()
    greet(barrier, near)

    def project(s, store):
        rows = rows_of(s)
        xp = product(tok[rows, :], pin[...])
        xp = jnp.concatenate([xp[: length // 2], xp[length // 2 :]], axis=1)
        gpt[s] = product(pout[...], og[rows, :])
        for q in range(nx):
            even = gpt[s, pl.ds(16 * q, 8, stride=2), :]
            odd = gpt[s, pl.ds(16 * q + 1, 8, stride=2), :]
            store(q, xp, jnp.concatenate([even, odd], axis=1))

    def store_last(q, xp, gq):
        mine_last[q, 0:32, :] = xp
        mine_last[q, 32:40, :] = gq

    for i in range(4):
        loads[i].wait()
    project(3, store_last)

    pl.semaphore_wait(barrier, len(near))
    for d in range(1, nx):
        pltpu.make_async_remote_copy(
            mine_last.at[x_peers[d - 1][1]], recv_last.at[nx - 1 - d], xl_send, xl_recv,
            device_id=x_peers[d - 1], device_id_type=MESH,
        ).start()
    greet(token_a, two_off)

    loads[4].wait()
    loads[5].wait()
    slots = [slot_of[src[i]] for i in range(4)]
    ids[0] = jnp.full((1, 128), slots[3], jnp.int32)

    def to_spread(source, target, send_sem, recv_sem):
        for t in range(1, len(spread)):
            dy, dc = spread[t]
            back = ((ny - dy) % ny) * CORES + dc
            pltpu.make_async_remote_copy(
                source.at[0], target.at[back], send_sem, recv_sem,
                device_id=spread_peers[t], device_id_type=MESH,
            ).start()

    to_spread(ids, ids, id_send, id_recv)

    loads[6].wait()
    loads[7].wait()
    for s in range(3):
        def store_rest(q, xp, gq):
            mine_rest[q, s, 0:32, :] = xp
            mine_rest[q, s, 32:40, :] = gq

        project(s, store_rest)
    for d in range(1, nx):
        pltpu.make_async_remote_copy(
            mine_rest.at[x_peers[d - 1][1]], recv_rest.at[nx - 1 - d], xr_send, xr_recv,
            device_id=x_peers[d - 1], device_id_type=MESH,
        ).start()

    pl.semaphore_wait(token_a, len(two_off))
    greet(token_b, four_off)

    low = lax.broadcasted_iota(jnp.int32, (32, 128), 1) < 64

    def sketch(total):
        xp, gq = total[0:32], total[32:40]
        turned = pltpu.roll(xp, 64, 1)
        twice = jnp.concatenate(
            [
                jnp.where(low, xp, 0.0), jnp.where(low, turned, 0.0),
                jnp.where(low, 0.0, turned), jnp.where(low, 0.0, xp),
            ],
            axis=0,
        )
        value = lax.dot_general(
            gq, twice, (((1,), (0,)), ((), ())),
            precision=lax.Precision.HIGHEST, preferred_element_type=F32,
        )
        return value * (length ** -0.5)

    pltpu.make_async_copy(recv_last, recv_last, xl_recv).wait()
    total = mine_last[m]
    for d in range(nx - 1):
        total = total + recv_last[d]
    held[0] = sketch(total)
    to_spread(held, held, held_send, held_recv)

    others = pl.ds(1, len(spread) - 1)
    pltpu.make_async_copy(ids.at[others], ids.at[others], id_recv).wait()
    if four_off:
        pl.semaphore_wait(token_b, len(four_off))
    pltpu.make_async_copy(held.at[others], held.at[others], held_recv).wait()

    def owner_rows(zz):
        base = dp_of(y, zz, core) * 2
        rows = []
        for w in range(2):
            acc = jnp.zeros((8, 128), F32)
            for i in range(len(spread)):
                acc = acc + jnp.where(ids[i] == base + w, held[i], 0.0)
            rows.append(acc)
        return rows

    for k in range(nz - 1):
        zz = k + lax.div(nz + k - z, nz)
        for w, row in enumerate(owner_rows(zz)):
            z_out[k, w] = row
        pltpu.make_async_remote_copy(
            z_out.at[k], z_in.at[lax.rem(z - zz + nz, nz)], z_send, z_recv,
            device_id=(dp_of(y, zz, core), m), device_id_type=MESH,
        ).start()
    for w, row in enumerate(owner_rows(z)):
        z_in[0, w] = row

    pltpu.make_async_copy(recv_rest, recv_rest, xr_recv).wait()
    for s in range(3):
        total = mine_rest[m, s]
        for d in range(nx - 1):
            total = total + recv_rest[d, s]
        value = sketch(total)
        for w in range(2):
            weight = jnp.where(slots[s] == fixed_to[s] * 2 + w, 1.0, 0.0).astype(F32)
            fixed_out[s, w] = value * weight
        pltpu.make_async_remote_copy(
            fixed_out.at[s], fixed_in.at[s], fixed_send.at[s], fixed_recv.at[s],
            device_id=(fixed_to[s], m), device_id_type=MESH,
        ).start()

    for s in range(3):
        pltpu.make_async_copy(fixed_in.at[s], fixed_in.at[s], fixed_recv.at[s]).wait()
    landed = z_in.at[pl.ds(1, nz - 1)]
    pltpu.make_async_copy(landed, landed, z_recv).wait()
    for w in range(2):
        acc = z_in[0, w]
        for s in range(3):
            acc = acc + fixed_in[s, w]
        for t in range(1, nz):
            acc = acc + z_in[t, w]
        out_ref[w] = acc

    pltpu.make_async_copy(recv_last, recv_last, xl_send).wait()
    pltpu.make_async_copy(recv_rest, recv_rest, xr_send).wait()
    pltpu.make_async_copy(ids.at[others], ids.at[others], id_send).wait()
    pltpu.make_async_copy(held.at[others], held.at[others], held_send).wait()
    for s in range(3):
        pltpu.make_async_copy(fixed_out.at[s], fixed_out.at[s], fixed_send.at[s]).wait()
    pltpu.make_async_copy(landed, landed, z_send).wait()


def local(ny, nz, nx, tokens, out_grad, proj_in, proj_out, source_ids, slot_of_source):
    length = tokens.shape[0] // source_ids.shape[0]
    pin, pout = proj_in.T, proj_out.T
    spread = ny * CORES
    dma, regular = pltpu.SemaphoreType.DMA, pltpu.SemaphoreType.REGULAR
    out = pl.pallas_call(
        functools.partial(kernel, ny, nz, nx, length),
        out_shape=jax.ShapeDtypeStruct((2, 8, 128), F32),
        in_specs=[pl.BlockSpec(memory_space=pl.ANY)] * 6,
        out_specs=pl.BlockSpec(memory_space=pltpu.VMEM),
        scratch_shapes=[
            pltpu.VMEM(tokens.shape, tokens.dtype),
            pltpu.VMEM(out_grad.shape, out_grad.dtype),
            pltpu.VMEM(pin.shape, pin.dtype),
            pltpu.VMEM(pout.shape, pout.dtype),
            pltpu.SMEM(source_ids.shape, jnp.int32),
            pltpu.SMEM(slot_of_source.shape, jnp.int32),
            pltpu.VMEM((4, 64, length), F32),
            pltpu.VMEM((nx, PACKED, 128), F32),
            pltpu.VMEM((nx, 3, PACKED, 128), F32),
            pltpu.VMEM((nx - 1, PACKED, 128), F32),
            pltpu.VMEM((nx - 1, 3, PACKED, 128), F32),
            pltpu.VMEM((spread, 8, 128), F32),
            pltpu.VMEM((spread, 1, 128), jnp.int32),
            pltpu.VMEM((3, 2, 8, 128), F32),
            pltpu.VMEM((3, 2, 8, 128), F32),
            pltpu.VMEM((nz, 2, 8, 128), F32),
            pltpu.VMEM((nz, 2, 8, 128), F32),
            dma((8,)), dma, dma, dma, dma, dma, dma, dma, dma, dma((3,)), dma((3,)), dma, dma,
            regular, regular,
        ],
        compiler_params=pltpu.CompilerParams(
            collective_id=0, has_side_effects=True, vmem_limit_bytes=60 * 2**20
        ),
    )(tokens, out_grad, pin, pout, source_ids, slot_of_source)
    return out.reshape(2, 8 * 128)


def solution(mesh):
    nx, ndp = mesh.shape["tensor"], mesh.shape["dp"]
    ny = COLUMNS
    nz = ndp // (ny * CORES)
    placed = (
        P("dp", "tensor"),
        P("dp", "tensor"),
        P("tensor", None),
        P("tensor", None),
        P("dp"),
        P(),
    )
    return jax.shard_map(
        functools.partial(local, ny, nz, nx),
        mesh=mesh, in_specs=placed, out_specs=P("dp", "tensor"), check_vma=False,
    )
```

```python
import functools

import jax
import jax.numpy as jnp
from jax import lax
from jax.experimental import pallas as pl
from jax.experimental.pallas import tpu as pltpu
from jax.sharding import PartitionSpec as P

MESH = pl.DeviceIdType.MESH
F32 = jnp.float32
CORES = 2
COLUMNS = 4
PACKED = 40


def away(d, n):
    return min(d, n - d)


def product(a, b):
    return lax.dot_general(a, b, (((1,), (1,)), ((), ())), preferred_element_type=F32)


def kernel(
    ny, nz, nx, length,
    tok_hbm, og_hbm, pin_hbm, pout_hbm, src_hbm, slot_hbm,
    out_ref,
    tok, og, pin, pout, src, slot_of, gpt,
    mine_last, mine_rest, recv_last, recv_rest,
    held, ids, fixed_out, fixed_in, z_out, z_in,
    load_sem, xl_send, xl_recv, xr_send, xr_recv,
    id_send, id_recv, held_send, held_recv,
    fixed_send, fixed_recv, z_send, z_recv, token_a, token_b,
):
    j = lax.axis_index("dp")
    m = lax.axis_index("tensor")
    ndp = ny * nz * CORES
    half = ndp // 2
    core = lax.rem(j, CORES)
    z = lax.rem(lax.div(j, CORES), nz)
    y = lax.div(j, CORES * nz)

    def dp_of(yy, zz, cc):
        return (yy * nz + zz) * CORES + cc

    def rows_of(s):
        return pl.ds(s * length, length)

    last, rest = rows_of(3), pl.ds(0, 3 * length)
    loads = [
        (pout_hbm, pout),
        (og_hbm.at[last], og.at[last]),
        (pin_hbm, pin),
        (tok_hbm.at[last], tok.at[last]),
        (src_hbm, src),
        (slot_hbm, slot_of),
        (og_hbm.at[rest], og.at[rest]),
        (tok_hbm.at[rest], tok.at[rest]),
    ]
    loads = [pltpu.make_async_copy(a, b, load_sem.at[i]) for i, (a, b) in enumerate(loads)]
    for load in loads:
        load.start()

    def z_peers(offsets):
        offsets = sorted({d % nz for d in offsets} - {0})
        return [(dp_of(y, lax.rem(z + d, nz), core), m) for d in offsets]

    def greet(sem, peers):
        for peer in peers:
            pl.semaphore_signal(sem, inc=1, device_id=peer, device_id_type=MESH)

    x_peers = [(j, lax.rem(m + d, nx)) for d in range(1, nx)]
    spread = [(dy, dc) for dy in range(ny) for dc in range(CORES)]
    spread_peers = [
        (dp_of(lax.rem(y + dy, ny), z, lax.rem(core + dc, CORES)), m) for dy, dc in spread
    ]
    x_order = sorted(range(1, nx), key=lambda d: -away(d, nx))
    spread_order = sorted(
        range(1, len(spread)), key=lambda t: (-away(spread[t][0], ny), -spread[t][1])
    )
    fixed_to = [lax.rem(j + ndp - 1, ndp), lax.rem(j + 1, ndp), lax.rem(j + half, ndp)]
    beside = lax.rem(j + ndp + 2 * core - 1, ndp)
    near = x_peers + spread_peers[1:] + z_peers((1, 2, -1, -2)) + [(beside, m)]
    two_off, four_off = z_peers((2, -2)), z_peers((4, -4))
    barrier = pltpu.get_barrier_semaphore()
    greet(barrier, near)

    def project(s, store):
        rows = rows_of(s)
        xp = product(tok[rows, :], pin[...])
        xp = jnp.concatenate([xp[: length // 2], xp[length // 2 :]], axis=1)
        gpt[s] = product(pout[...], og[rows, :])
        for q in range(nx):
            even = gpt[s, pl.ds(16 * q, 8, stride=2), :]
            odd = gpt[s, pl.ds(16 * q + 1, 8, stride=2), :]
            store(q, xp, jnp.concatenate([even, odd], axis=1))

    def store_last(q, xp, gq):
        mine_last[q, 0:32, :] = xp
        mine_last[q, 32:40, :] = gq

    for i in range(4):
        loads[i].wait()
    project(3, store_last)

    pl.semaphore_wait(barrier, len(near))
    for d in x_order:
        pltpu.make_async_remote_copy(
            mine_last.at[x_peers[d - 1][1]], recv_last.at[nx - 1 - d], xl_send, xl_recv,
            device_id=x_peers[d - 1], device_id_type=MESH,
        ).start()
    greet(token_a, two_off)

    loads[4].wait()
    loads[5].wait()
    slots = [slot_of[src[i]] for i in range(4)]
    ids[0] = jnp.full((1, 128), slots[3], jnp.int32)

    def to_spread(source, target, send_sem, recv_sem):
        for t in spread_order:
            dy, dc = spread[t]
            back = ((ny - dy) % ny) * CORES + dc
            pltpu.make_async_remote_copy(
                source.at[0], target.at[back], send_sem, recv_sem,
                device_id=spread_peers[t], device_id_type=MESH,
            ).start()

    to_spread(ids, ids, id_send, id_recv)

    loads[6].wait()
    loads[7].wait()
    for s in range(3):
        def store_rest(q, xp, gq):
            mine_rest[q, s, 0:32, :] = xp
            mine_rest[q, s, 32:40, :] = gq

        project(s, store_rest)
    pl.semaphore_wait(token_a, len(two_off))
    greet(token_b, four_off)

    for d in x_order:
        pltpu.make_async_remote_copy(
            mine_rest.at[x_peers[d - 1][1]], recv_rest.at[nx - 1 - d], xr_send, xr_recv,
            device_id=x_peers[d - 1], device_id_type=MESH,
        ).start()

    low = lax.broadcasted_iota(jnp.int32, (32, 128), 1) < 64

    def sketch(total):
        xp, gq = total[0:32], total[32:40]
        turned = pltpu.roll(xp, 64, 1)
        twice = jnp.concatenate(
            [
                jnp.where(low, xp, 0.0), jnp.where(low, turned, 0.0),
                jnp.where(low, 0.0, turned), jnp.where(low, 0.0, xp),
            ],
            axis=0,
        )
        value = lax.dot_general(
            gq, twice, (((1,), (0,)), ((), ())),
            precision=lax.Precision.HIGHEST, preferred_element_type=F32,
        )
        return value * (length ** -0.5)

    pltpu.make_async_copy(recv_last, recv_last, xl_recv).wait()
    total = mine_last[m]
    for d in range(nx - 1):
        total = total + recv_last[d]
    held[0] = sketch(total)
    to_spread(held, held, held_send, held_recv)

    others = pl.ds(1, len(spread) - 1)
    pltpu.make_async_copy(ids.at[others], ids.at[others], id_recv).wait()
    if four_off:
        pl.semaphore_wait(token_b, len(four_off))
    pltpu.make_async_copy(held.at[others], held.at[others], held_recv).wait()

    def owner_rows(zz):
        base = dp_of(y, zz, core) * 2
        rows = []
        for w in range(2):
            acc = jnp.zeros((8, 128), F32)
            for i in range(len(spread)):
                acc = acc + jnp.where(ids[i] == base + w, held[i], 0.0)
            rows.append(acc)
        return rows

    for k in range(nz - 1):
        zz = k + lax.div(nz + k - z, nz)
        for w, row in enumerate(owner_rows(zz)):
            z_out[k, w] = row
        pltpu.make_async_remote_copy(
            z_out.at[k], z_in.at[lax.rem(z - zz + nz, nz)], z_send, z_recv,
            device_id=(dp_of(y, zz, core), m), device_id_type=MESH,
        ).start()
    for w, row in enumerate(owner_rows(z)):
        z_in[0, w] = row

    pltpu.make_async_copy(recv_rest, recv_rest, xr_recv).wait()
    for s in range(3):
        total = mine_rest[m, s]
        for d in range(nx - 1):
            total = total + recv_rest[d, s]
        value = sketch(total)
        for w in range(2):
            weight = jnp.where(slots[s] == fixed_to[s] * 2 + w, 1.0, 0.0).astype(F32)
            fixed_out[s, w] = value * weight
        pltpu.make_async_remote_copy(
            fixed_out.at[s], fixed_in.at[s], fixed_send.at[s], fixed_recv.at[s],
            device_id=(fixed_to[s], m), device_id_type=MESH,
        ).start()

    for s in range(3):
        pltpu.make_async_copy(fixed_in.at[s], fixed_in.at[s], fixed_recv.at[s]).wait()
    landed = z_in.at[pl.ds(1, nz - 1)]
    pltpu.make_async_copy(landed, landed, z_recv).wait()
    for w in range(2):
        acc = z_in[0, w]
        for s in range(3):
            acc = acc + fixed_in[s, w]
        for t in range(1, nz):
            acc = acc + z_in[t, w]
        out_ref[w] = acc

    pltpu.make_async_copy(recv_last, recv_last, xl_send).wait()
    pltpu.make_async_copy(recv_rest, recv_rest, xr_send).wait()
    pltpu.make_async_copy(ids.at[others], ids.at[others], id_send).wait()
    pltpu.make_async_copy(held.at[others], held.at[others], held_send).wait()
    for s in range(3):
        pltpu.make_async_copy(fixed_out.at[s], fixed_out.at[s], fixed_send.at[s]).wait()
    pltpu.make_async_copy(landed, landed, z_send).wait()


def local(ny, nz, nx, tokens, out_grad, proj_in, proj_out, source_ids, slot_of_source):
    length = tokens.shape[0] // source_ids.shape[0]
    pin, pout = proj_in.T, proj_out.T
    spread = ny * CORES
    dma, regular = pltpu.SemaphoreType.DMA, pltpu.SemaphoreType.REGULAR
    out = pl.pallas_call(
        functools.partial(kernel, ny, nz, nx, length),
        out_shape=pltpu.VMEM((2, 8, 128), F32),
        in_specs=[pl.BlockSpec(memory_space=pl.ANY)] * 6,
        out_specs=pl.BlockSpec(memory_space=pltpu.VMEM),
        scratch_shapes=[
            pltpu.VMEM(tokens.shape, tokens.dtype),
            pltpu.VMEM(out_grad.shape, out_grad.dtype),
            pltpu.VMEM(pin.shape, pin.dtype),
            pltpu.VMEM(pout.shape, pout.dtype),
            pltpu.SMEM(source_ids.shape, jnp.int32),
            pltpu.SMEM(slot_of_source.shape, jnp.int32),
            pltpu.VMEM((4, 64, length), F32),
            pltpu.VMEM((nx, PACKED, 128), F32),
            pltpu.VMEM((nx, 3, PACKED, 128), F32),
            pltpu.VMEM((nx - 1, PACKED, 128), F32),
            pltpu.VMEM((nx - 1, 3, PACKED, 128), F32),
            pltpu.VMEM((spread, 8, 128), F32),
            pltpu.VMEM((spread, 1, 128), jnp.int32),
            pltpu.VMEM((3, 2, 8, 128), F32),
            pltpu.VMEM((3, 2, 8, 128), F32),
            pltpu.VMEM((nz, 2, 8, 128), F32),
            pltpu.VMEM((nz, 2, 8, 128), F32),
            dma((8,)), dma, dma, dma, dma, dma, dma, dma, dma, dma((3,)), dma((3,)), dma, dma,
            regular, regular,
        ],
        compiler_params=pltpu.CompilerParams(
            collective_id=0, has_side_effects=True, vmem_limit_bytes=60 * 2**20
        ),
    )(tokens, out_grad, pin, pout, source_ids, slot_of_source)
    return out.reshape(2, 8 * 128)


def solution(mesh):
    nx, ndp = mesh.shape["tensor"], mesh.shape["dp"]
    ny = COLUMNS
    nz = ndp // (ny * CORES)
    placed = (
        P("dp", "tensor"),
        P("dp", "tensor"),
        P("tensor", None),
        P("tensor", None),
        P("dp"),
        P(),
    )
    return jax.shard_map(
        functools.partial(local, ny, nz, nx),
        mesh=mesh, in_specs=placed, out_specs=P("dp", "tensor"), check_vma=False,
    )
```

```python
import functools

import jax
import jax.numpy as jnp
from jax import lax
from jax.experimental import pallas as pl
from jax.experimental.pallas import tpu as pltpu
from jax.sharding import PartitionSpec as P

MESH = pl.DeviceIdType.MESH
F32 = jnp.float32
CORES = 2
COLUMNS = 4
HEADS = 5
FIRST = ((0, 1),)
PACKED = 40


def away(d, n):
    return min(d, n - d)


def product(a, b):
    return lax.dot_general(a, b, (((1,), (1,)), ((), ())), preferred_element_type=F32)


def kernel(
    ny, nz, nx, length,
    tok_hbm, og_hbm, pin_hbm, pout_hbm, src_hbm, slot_hbm,
    out_ref,
    tok, og, pin, pout, src, slot_of, gpt,
    mine_last, mine_rest, recv_last, recv_rest,
    held, ids, fixed_out, fixed_in, y_out, y_in,
    straight, straight_ids, straight_send, straight_recv, straight_id_send, straight_id_recv,
    load_sem, xl_send, xl_recv, xr_send, xr_recv,
    id_send, id_recv, held_send, held_recv,
    fixed_send, fixed_recv, y_send, y_recv, token_a, token_b,
):
    j = lax.axis_index("dp")
    m = lax.axis_index("tensor")
    ndp = ny * nz * CORES
    half = ndp // 2
    core = lax.rem(j, CORES)
    z = lax.rem(lax.div(j, CORES), nz)
    y = lax.div(j, CORES * nz)

    def dp_of(yy, zz, cc):
        return (yy * nz + zz) * CORES + cc

    def rows_of(s):
        return pl.ds(s * length, length)

    last, rest = rows_of(3), pl.ds(0, 3 * length)
    loads = [
        (pout_hbm, pout),
        (og_hbm.at[last], og.at[last]),
        (pin_hbm, pin),
        (tok_hbm.at[last], tok.at[last]),
        (src_hbm, src),
        (slot_hbm, slot_of),
        (og_hbm.at[rest], og.at[rest]),
        (tok_hbm.at[rest], tok.at[rest]),
    ]
    loads = [pltpu.make_async_copy(a, b, load_sem.at[i]) for i, (a, b) in enumerate(loads)]
    for load in loads:
        load.start()

    def z_peers(offsets):
        offsets = sorted({d % nz for d in offsets} - {0})
        return [(dp_of(y, lax.rem(z + d, nz), core), m) for d in offsets]

    def greet(sem, peers):
        for peer in peers:
            pl.semaphore_signal(sem, inc=1, device_id=peer, device_id_type=MESH)

    x_peers = [(j, lax.rem(m + d, nx)) for d in range(1, nx)]
    spread = [(dy, dc) for dy in range(ny) for dc in range(CORES)]
    spread_peers = [
        (dp_of(lax.rem(y + dy, ny), z, lax.rem(core + dc, CORES)), m) for dy, dc in spread
    ]
    x_order = sorted(range(1, nx), key=lambda d: -away(d, nx))
    spread_order = sorted(
        range(1, len(spread)), key=lambda t: (-away(spread[t][0], ny), -spread[t][1])
    )
    fixed_to = [lax.rem(j + ndp - 1, ndp), lax.rem(j + 1, ndp), lax.rem(j + half, ndp)]
    beside = lax.rem(j + ndp + 2 * core - 1, ndp)
    near = x_peers + spread_peers[1:] + z_peers((1, 2, -1, -2)) + [(beside, m)]
    two_off, four_off = z_peers((2, -2)), z_peers((4, -4))
    barrier = pltpu.get_barrier_semaphore()
    greet(barrier, near)
    heads = HEADS if nz >= 16 else 0

    @pl.when(z < heads)
    def _():
        greet(barrier, z_peers(range(1, nz)))

    far = range(nz // 2 - 1, nz // 2 + 4) if heads else range(0)
    firsts = FIRST if heads else ()
    is_far = jnp.logical_and(z >= nz // 2 - 1, z <= nz // 2 + 3)
    far_group = lax.div(z + nz // 2 + 1, nz) - lax.div(z + nz // 2 - 4, nz)

    def at_first(yy, cc):
        at = z < 0
        for fy, fc in firsts:
            at = jnp.logical_or(at, jnp.logical_and(yy == fy, cc == fc))
        return at

    is_first = jnp.logical_and(z == 0, at_first(y, core))

    @pl.when(is_first)
    def _():
        for zz in far:
            greet(barrier, [(dp_of(yy, zz, cc), m) for yy in range(ny) for cc in range(CORES)])


    def project(s, store):
        rows = rows_of(s)
        xp = product(tok[rows, :], pin[...])
        xp = jnp.concatenate([xp[: length // 2], xp[length // 2 :]], axis=1)
        gpt[s] = product(pout[...], og[rows, :])
        for q in range(nx):
            even = gpt[s, pl.ds(16 * q, 8, stride=2), :]
            odd = gpt[s, pl.ds(16 * q + 1, 8, stride=2), :]
            store(q, xp, jnp.concatenate([even, odd], axis=1))

    def store_last(q, xp, gq):
        mine_last[q, 0:32, :] = xp
        mine_last[q, 32:40, :] = gq

    for i in range(4):
        loads[i].wait()
    project(3, store_last)

    @pl.when(z < heads)
    def _():
        pl.semaphore_wait(barrier, len(near) + heads - 1)

    @pl.when(jnp.logical_and(z >= heads, jnp.logical_not(is_far)))
    def _():
        pl.semaphore_wait(barrier, len(near) + heads)

    if heads:
        @pl.when(is_far)
        def _():
            pl.semaphore_wait(barrier, len(near) + heads + len(firsts))

    for d in x_order:
        pltpu.make_async_remote_copy(
            mine_last.at[x_peers[d - 1][1]], recv_last.at[nx - 1 - d], xl_send, xl_recv,
            device_id=x_peers[d - 1], device_id_type=MESH,
        ).start()
    greet(token_a, two_off)

    loads[4].wait()
    loads[5].wait()
    slots = [slot_of[src[i]] for i in range(4)]
    ids[0] = jnp.full((1, 128), slots[3], jnp.int32)

    def along_z(source, targets, send_sem, recv_sem):
        for zz in targets:
            @pl.when(z != zz)
            def _():
                pltpu.make_async_remote_copy(
                    source.at[0], source.at[lax.rem(z - zz + nz, nz)], send_sem, recv_sem,
                    device_id=(dp_of(y, zz, core), m), device_id_type=MESH,
                ).start()

    def to_first(source, target, send_sem, recv_sem):
        if not firsts:
            return

        @pl.when(is_far)
        def _():
            for fy, fc in firsts:
                pltpu.make_async_remote_copy(
                    source.at[0], target.at[z - far[0], y * CORES + core], send_sem, recv_sem,
                    device_id=(dp_of(fy, 0, fc), m), device_id_type=MESH,
                ).start()

    early, late = range(heads), range(heads, nz)
    to_first(ids, straight_ids, straight_id_send, straight_id_recv)
    along_z(ids, early, id_send, id_recv)

    loads[6].wait()
    loads[7].wait()
    for s in range(3):
        def store_rest(q, xp, gq):
            mine_rest[q, s, 0:32, :] = xp
            mine_rest[q, s, 32:40, :] = gq

        project(s, store_rest)
    pl.semaphore_wait(token_a, len(two_off))
    greet(token_b, four_off)

    for d in x_order:
        pltpu.make_async_remote_copy(
            mine_rest.at[x_peers[d - 1][1]], recv_rest.at[nx - 1 - d], xr_send, xr_recv,
            device_id=x_peers[d - 1], device_id_type=MESH,
        ).start()

    low = lax.broadcasted_iota(jnp.int32, (32, 128), 1) < 64

    def sketch(total):
        xp, gq = total[0:32], total[32:40]
        turned = pltpu.roll(xp, 64, 1)
        twice = jnp.concatenate(
            [
                jnp.where(low, xp, 0.0), jnp.where(low, turned, 0.0),
                jnp.where(low, 0.0, turned), jnp.where(low, 0.0, xp),
            ],
            axis=0,
        )
        value = lax.dot_general(
            gq, twice, (((1,), (0,)), ((), ())),
            precision=lax.Precision.HIGHEST, preferred_element_type=F32,
        )
        return value * (length ** -0.5)

    pltpu.make_async_copy(recv_last, recv_last, xl_recv).wait()
    total = mine_last[m]
    for d in range(nx - 1):
        total = total + recv_last[d]
    held[0] = sketch(total)
    to_first(held, straight, straight_send, straight_recv)
    along_z(held, early, held_send, held_recv.at[far_group])
    if four_off:
        pl.semaphore_wait(token_b, len(four_off))
    along_z(ids, late, id_send, id_recv)
    along_z(held, late, held_send, held_recv.at[far_group])

    pltpu.make_async_copy(recv_rest, recv_rest, xr_recv).wait()
    for s in range(3):
        total = mine_rest[m, s]
        for d in range(nx - 1):
            total = total + recv_rest[d, s]
        value = sketch(total)
        for w in range(2):
            weight = jnp.where(slots[s] == fixed_to[s] * 2 + w, 1.0, 0.0).astype(F32)
            fixed_out[s, w] = value * weight
        pltpu.make_async_remote_copy(
            fixed_out.at[s], fixed_in.at[s], fixed_send.at[s], fixed_recv.at[s],
            device_id=(fixed_to[s], m), device_id_type=MESH,
        ).start()

    others = pl.ds(1, nz - 1)
    pltpu.make_async_copy(ids.at[others], ids.at[others], id_recv).wait()

    def arrived(count, group):
        slots = held.at[pl.ds(0, count)]
        pltpu.make_async_copy(slots, slots, held_recv.at[group]).wait()

    def add(t, slots, fresh):
        base = spread_peers[t][0] * 2
        for w in range(2):
            acc = jnp.zeros((8, 128), F32) if fresh else y_out[t, w]
            for i in slots:
                acc = acc + jnp.where(ids[i] == base + w, held[i], 0.0)
            y_out[t, w] = acc

    def to_spread(t):
        if t:
            dy, dc = spread[t]
            back = ((ny - dy) % ny) * CORES + dc
            pltpu.make_async_remote_copy(
                y_out.at[t], y_in.at[back], y_send, y_recv,
                device_id=spread_peers[t], device_id_type=MESH,
            ).start()

    def goes_first(t):
        dy, dc = spread[t]
        return at_first(lax.rem(y + dy, ny), lax.rem(core + dc, CORES))

    if heads:
        @pl.when(z == 0)
        def _():
            arrived(nz - 1 - len(far), 0)
            for t in spread_order + [0]:
                add(t, [i for i in range(nz) if i not in far], True)

                @pl.when(goes_first(t))
                def _():
                    to_spread(t)

            arrived(len(far), 1)
            for t in spread_order + [0]:
                @pl.when(jnp.logical_not(goes_first(t)))
                def _():
                    add(t, far, False)
                    to_spread(t)

    @pl.when(z >= (1 if heads else 0))
    def _():
        if heads:
            @pl.when(is_far)
            def _():
                arrived(nz - len(far), 0)
                arrived(len(far) - 1, 1)

            @pl.when(jnp.logical_not(is_far))
            def _():
                arrived(nz - 1 - len(far), 0)
                arrived(len(far), 1)
        else:
            arrived(nz - 1, 0)
        for t in spread_order + [0]:
            add(t, range(nz), True)
            to_spread(t)

    for s in range(3):
        pltpu.make_async_copy(fixed_in.at[s], fixed_in.at[s], fixed_recv.at[s]).wait()
    landed = y_in.at[pl.ds(1, len(spread) - 1)]
    pltpu.make_async_copy(landed, landed, y_recv).wait()
    for w in range(2):
        acc = y_out[0, w]
        for s in range(3):
            acc = acc + fixed_in[s, w]
        for t in range(1, len(spread)):
            acc = acc + y_in[t, w]
        out_ref[w] = acc

    if firsts:
        @pl.when(is_first)
        def _():
            for buffer, sem in ((straight_ids, straight_id_recv), (straight, straight_recv)):
                pltpu.make_async_copy(buffer, buffer, sem).wait()
            for w in range(2):
                acc = out_ref[w]
                for i in range(len(far)):
                    for t in range(len(spread)):
                        acc = acc + jnp.where(straight_ids[i, t] == j * 2 + w, straight[i, t], 0.0)
                out_ref[w] = acc

        @pl.when(is_far)
        def _():
            for buffer, sem in ((straight_ids, straight_id_send), (straight, straight_send)):
                sent = buffer.at[0, pl.ds(0, len(firsts))]
                pltpu.make_async_copy(sent, sent, sem).wait()

    pltpu.make_async_copy(recv_last, recv_last, xl_send).wait()
    pltpu.make_async_copy(recv_rest, recv_rest, xr_send).wait()
    pltpu.make_async_copy(ids.at[others], ids.at[others], id_send).wait()
    pltpu.make_async_copy(held.at[others], held.at[others], held_send).wait()
    for s in range(3):
        pltpu.make_async_copy(fixed_out.at[s], fixed_out.at[s], fixed_send.at[s]).wait()
    pltpu.make_async_copy(landed, landed, y_send).wait()


def local(ny, nz, nx, tokens, out_grad, proj_in, proj_out, source_ids, slot_of_source):
    length = tokens.shape[0] // source_ids.shape[0]
    pin, pout = proj_in.T, proj_out.T
    spread = ny * CORES
    dma, regular = pltpu.SemaphoreType.DMA, pltpu.SemaphoreType.REGULAR
    out = pl.pallas_call(
        functools.partial(kernel, ny, nz, nx, length),
        out_shape=pltpu.VMEM((2, 8, 128), F32),
        in_specs=[pl.BlockSpec(memory_space=pl.ANY)] * 6,
        out_specs=pl.BlockSpec(memory_space=pltpu.VMEM),
        scratch_shapes=[
            pltpu.VMEM(tokens.shape, tokens.dtype),
            pltpu.VMEM(out_grad.shape, out_grad.dtype),
            pltpu.VMEM(pin.shape, pin.dtype),
            pltpu.VMEM(pout.shape, pout.dtype),
            pltpu.SMEM(source_ids.shape, jnp.int32),
            pltpu.SMEM(slot_of_source.shape, jnp.int32),
            pltpu.VMEM((4, 64, length), F32),
            pltpu.VMEM((nx, PACKED, 128), F32),
            pltpu.VMEM((nx, 3, PACKED, 128), F32),
            pltpu.VMEM((nx - 1, PACKED, 128), F32),
            pltpu.VMEM((nx - 1, 3, PACKED, 128), F32),
            pltpu.VMEM((nz, 8, 128), F32),
            pltpu.VMEM((nz, 1, 128), jnp.int32),
            pltpu.VMEM((3, 2, 8, 128), F32),
            pltpu.VMEM((3, 2, 8, 128), F32),
            pltpu.VMEM((spread, 2, 8, 128), F32),
            pltpu.VMEM((spread, 2, 8, 128), F32),
            pltpu.VMEM((5, spread, 8, 128), F32),
            pltpu.VMEM((5, spread, 1, 128), jnp.int32),
            dma, dma, dma, dma,
            dma((8,)), dma, dma, dma, dma, dma, dma, dma, dma((2,)), dma((3,)), dma((3,)), dma, dma,
            regular, regular,
        ],
        compiler_params=pltpu.CompilerParams(
            collective_id=0, has_side_effects=True, vmem_limit_bytes=60 * 2**20
        ),
    )(tokens, out_grad, pin, pout, source_ids, slot_of_source)
    return out.reshape(2, 8 * 128)


def solution(mesh):
    nx, ndp = mesh.shape["tensor"], mesh.shape["dp"]
    ny = COLUMNS
    nz = ndp // (ny * CORES)
    placed = (
        P("dp", "tensor"),
        P("dp", "tensor"),
        P("tensor", None),
        P("tensor", None),
        P("dp"),
        P(),
    )
    return jax.shard_map(
        functools.partial(local, ny, nz, nx),
        mesh=mesh, in_specs=placed, out_specs=P("dp", "tensor"), check_vma=False,
    )
```

```python
import functools

import jax
import jax.numpy as jnp
from jax import lax
from jax.experimental import pallas as pl
from jax.experimental.pallas import tpu as pltpu
from jax.sharding import PartitionSpec as P

MESH = pl.DeviceIdType.MESH
F32 = jnp.float32
CORES = 2
COLUMNS = 4
HEADS = 5
FIRST = ((0, 1),)
FAR = 7
PACKED = 40


def away(d, n):
    return min(d, n - d)


def product(a, b):
    return lax.dot_general(a, b, (((1,), (1,)), ((), ())), preferred_element_type=F32)


def kernel(
    ny, nz, nx, length,
    tok_hbm, og_hbm, pin_hbm, pout_hbm, src_hbm, slot_hbm,
    out_ref,
    tok, og, pin, pout, src, slot_of, gpt,
    mine_last, mine_rest, recv_last, recv_rest,
    held, ids, fixed_out, fixed_in, y_out, y_in,
    straight, straight_ids, straight_send, straight_recv, straight_id_send, straight_id_recv,
    load_sem, xl_send, xl_recv, xr_send, xr_recv,
    id_send, id_recv, held_send, held_recv,
    fixed_send, fixed_recv, y_send, y_recv, token_a, token_b,
):
    j = lax.axis_index("dp")
    m = lax.axis_index("tensor")
    ndp = ny * nz * CORES
    half = ndp // 2
    core = lax.rem(j, CORES)
    z = lax.rem(lax.div(j, CORES), nz)
    y = lax.div(j, CORES * nz)

    def dp_of(yy, zz, cc):
        return (yy * nz + zz) * CORES + cc

    def rows_of(s):
        return pl.ds(s * length, length)

    last, rest = rows_of(3), pl.ds(0, 3 * length)
    loads = [
        (pout_hbm, pout),
        (og_hbm.at[last], og.at[last]),
        (pin_hbm, pin),
        (tok_hbm.at[last], tok.at[last]),
        (src_hbm, src),
        (slot_hbm, slot_of),
        (og_hbm.at[rest], og.at[rest]),
        (tok_hbm.at[rest], tok.at[rest]),
    ]
    loads = [pltpu.make_async_copy(a, b, load_sem.at[i]) for i, (a, b) in enumerate(loads)]
    for load in loads:
        load.start()

    def z_peers(offsets):
        offsets = sorted({d % nz for d in offsets} - {0})
        return [(dp_of(y, lax.rem(z + d, nz), core), m) for d in offsets]

    def greet(sem, peers):
        for peer in peers:
            pl.semaphore_signal(sem, inc=1, device_id=peer, device_id_type=MESH)

    x_peers = [(j, lax.rem(m + d, nx)) for d in range(1, nx)]
    spread = [(dy, dc) for dy in range(ny) for dc in range(CORES)]
    spread_peers = [
        (dp_of(lax.rem(y + dy, ny), z, lax.rem(core + dc, CORES)), m) for dy, dc in spread
    ]
    x_order = sorted(range(1, nx), key=lambda d: -away(d, nx))
    spread_order = sorted(
        range(1, len(spread)), key=lambda t: (-away(spread[t][0], ny), -spread[t][1])
    )
    fixed_to = [lax.rem(j + ndp - 1, ndp), lax.rem(j + 1, ndp), lax.rem(j + half, ndp)]
    beside = lax.rem(j + ndp + 2 * core - 1, ndp)
    near = x_peers + spread_peers[1:] + z_peers((1, 2, -1, -2)) + [(beside, m)]
    two_off, four_off = z_peers((2, -2)), z_peers((4, -4))
    barrier = pltpu.get_barrier_semaphore()
    greet(barrier, near)
    heads = HEADS if nz >= 16 else 0

    @pl.when(z < heads)
    def _():
        greet(barrier, z_peers(range(1, nz)))

    begin, end = nz // 2 - FAR // 2 + 1, nz // 2 + FAR // 2 + 2
    far = range(begin, end) if heads else range(0)
    firsts = FIRST if heads else ()
    is_far = jnp.logical_and(z >= begin, z < end)
    far_group = lax.div(z + nz - begin, nz) - lax.div(z + nz - end, nz)

    def at_first(yy, cc):
        at = z < 0
        for fy, fc in firsts:
            at = jnp.logical_or(at, jnp.logical_and(yy == fy, cc == fc))
        return at

    is_first = jnp.logical_and(z == 0, at_first(y, core))

    @pl.when(is_first)
    def _():
        for zz in far:
            greet(barrier, [(dp_of(yy, zz, cc), m) for yy in range(ny) for cc in range(CORES)])


    def project(s, store):
        rows = rows_of(s)
        xp = product(tok[rows, :], pin[...])
        xp = jnp.concatenate([xp[: length // 2], xp[length // 2 :]], axis=1)
        gpt[s] = product(pout[...], og[rows, :])
        for q in range(nx):
            even = gpt[s, pl.ds(16 * q, 8, stride=2), :]
            odd = gpt[s, pl.ds(16 * q + 1, 8, stride=2), :]
            store(q, xp, jnp.concatenate([even, odd], axis=1))

    def store_last(q, xp, gq):
        mine_last[q, 0:32, :] = xp
        mine_last[q, 32:40, :] = gq

    for i in range(4):
        loads[i].wait()
    project(3, store_last)

    @pl.when(z < heads)
    def _():
        pl.semaphore_wait(barrier, len(near) + heads - 1)

    @pl.when(jnp.logical_and(z >= heads, jnp.logical_not(is_far)))
    def _():
        pl.semaphore_wait(barrier, len(near) + heads)

    if heads:
        @pl.when(is_far)
        def _():
            pl.semaphore_wait(barrier, len(near) + heads + len(firsts))

    for d in x_order:
        pltpu.make_async_remote_copy(
            mine_last.at[x_peers[d - 1][1]], recv_last.at[nx - 1 - d], xl_send, xl_recv,
            device_id=x_peers[d - 1], device_id_type=MESH,
        ).start()
    greet(token_a, two_off)

    loads[4].wait()
    loads[5].wait()
    slots = [slot_of[src[i]] for i in range(4)]
    ids[0] = jnp.full((1, 128), slots[3], jnp.int32)

    def along_z(source, targets, send_sem, recv_sem):
        for zz in targets:
            @pl.when(z != zz)
            def _():
                pltpu.make_async_remote_copy(
                    source.at[0], source.at[lax.rem(z - zz + nz, nz)], send_sem, recv_sem,
                    device_id=(dp_of(y, zz, core), m), device_id_type=MESH,
                ).start()

    def to_first(source, target, send_sem, recv_sem):
        if not firsts:
            return

        @pl.when(is_far)
        def _():
            for fy, fc in firsts:
                pltpu.make_async_remote_copy(
                    source.at[0], target.at[z - far[0], y * CORES + core], send_sem, recv_sem,
                    device_id=(dp_of(fy, 0, fc), m), device_id_type=MESH,
                ).start()

    early, late = range(heads), range(heads, nz)
    to_first(ids, straight_ids, straight_id_send, straight_id_recv)
    along_z(ids, early, id_send, id_recv)

    loads[6].wait()
    loads[7].wait()
    for s in range(3):
        def store_rest(q, xp, gq):
            mine_rest[q, s, 0:32, :] = xp
            mine_rest[q, s, 32:40, :] = gq

        project(s, store_rest)
    pl.semaphore_wait(token_a, len(two_off))
    greet(token_b, four_off)

    for d in x_order:
        pltpu.make_async_remote_copy(
            mine_rest.at[x_peers[d - 1][1]], recv_rest.at[nx - 1 - d], xr_send, xr_recv,
            device_id=x_peers[d - 1], device_id_type=MESH,
        ).start()

    low = lax.broadcasted_iota(jnp.int32, (32, 128), 1) < 64

    def sketch(total):
        xp, gq = total[0:32], total[32:40]
        turned = pltpu.roll(xp, 64, 1)
        twice = jnp.concatenate(
            [
                jnp.where(low, xp, 0.0), jnp.where(low, turned, 0.0),
                jnp.where(low, 0.0, turned), jnp.where(low, 0.0, xp),
            ],
            axis=0,
        )
        value = lax.dot_general(
            gq, twice, (((1,), (0,)), ((), ())),
            precision=lax.Precision.HIGHEST, preferred_element_type=F32,
        )
        return value * (length ** -0.5)

    pltpu.make_async_copy(recv_last, recv_last, xl_recv).wait()
    total = mine_last[m]
    for d in range(nx - 1):
        total = total + recv_last[d]
    held[0] = sketch(total)
    along_z(held, range(1), held_send, held_recv.at[far_group])
    to_first(held, straight, straight_send, straight_recv)
    along_z(held, range(1, heads), held_send, held_recv.at[far_group])
    if four_off:
        pl.semaphore_wait(token_b, len(four_off))
    along_z(ids, late, id_send, id_recv)
    along_z(held, late, held_send, held_recv.at[far_group])

    pltpu.make_async_copy(recv_rest, recv_rest, xr_recv).wait()
    for s in range(3):
        total = mine_rest[m, s]
        for d in range(nx - 1):
            total = total + recv_rest[d, s]
        value = sketch(total)
        for w in range(2):
            weight = jnp.where(slots[s] == fixed_to[s] * 2 + w, 1.0, 0.0).astype(F32)
            fixed_out[s, w] = value * weight
        pltpu.make_async_remote_copy(
            fixed_out.at[s], fixed_in.at[s], fixed_send.at[s], fixed_recv.at[s],
            device_id=(fixed_to[s], m), device_id_type=MESH,
        ).start()

    others = pl.ds(1, nz - 1)
    pltpu.make_async_copy(ids.at[others], ids.at[others], id_recv).wait()

    def arrived(count, group):
        slots = held.at[pl.ds(0, count)]
        pltpu.make_async_copy(slots, slots, held_recv.at[group]).wait()

    def add(t, slots, fresh):
        base = spread_peers[t][0] * 2
        for w in range(2):
            acc = jnp.zeros((8, 128), F32) if fresh else y_out[t, w]
            for i in slots:
                acc = acc + jnp.where(ids[i] == base + w, held[i], 0.0)
            y_out[t, w] = acc

    def to_spread(t):
        if t:
            dy, dc = spread[t]
            back = ((ny - dy) % ny) * CORES + dc
            pltpu.make_async_remote_copy(
                y_out.at[t], y_in.at[back], y_send, y_recv,
                device_id=spread_peers[t], device_id_type=MESH,
            ).start()

    def goes_first(t):
        dy, dc = spread[t]
        return at_first(lax.rem(y + dy, ny), lax.rem(core + dc, CORES))

    if heads:
        @pl.when(z == 0)
        def _():
            arrived(nz - 1 - len(far), 0)
            for t in spread_order + [0]:
                add(t, [i for i in range(nz) if i not in far], True)

                @pl.when(goes_first(t))
                def _():
                    to_spread(t)

            arrived(len(far), 1)
            for t in spread_order + [0]:
                @pl.when(jnp.logical_not(goes_first(t)))
                def _():
                    add(t, far, False)
                    to_spread(t)

    @pl.when(z >= (1 if heads else 0))
    def _():
        if heads:
            @pl.when(is_far)
            def _():
                arrived(nz - len(far), 0)
                arrived(len(far) - 1, 1)

            @pl.when(jnp.logical_not(is_far))
            def _():
                arrived(nz - 1 - len(far), 0)
                arrived(len(far), 1)
        else:
            arrived(nz - 1, 0)
        for t in spread_order + [0]:
            add(t, range(nz), True)
            to_spread(t)

    for s in range(3):
        pltpu.make_async_copy(fixed_in.at[s], fixed_in.at[s], fixed_recv.at[s]).wait()
    landed = y_in.at[pl.ds(1, len(spread) - 1)]
    pltpu.make_async_copy(landed, landed, y_recv).wait()
    for w in range(2):
        acc = y_out[0, w]
        for s in range(3):
            acc = acc + fixed_in[s, w]
        for t in range(1, len(spread)):
            acc = acc + y_in[t, w]
        out_ref[w] = acc

    if firsts:
        @pl.when(is_first)
        def _():
            for buffer, sem in ((straight_ids, straight_id_recv), (straight, straight_recv)):
                pltpu.make_async_copy(buffer, buffer, sem).wait()
            for w in range(2):
                acc = out_ref[w]
                for i in range(len(far)):
                    for t in range(len(spread)):
                        acc = acc + jnp.where(straight_ids[i, t] == j * 2 + w, straight[i, t], 0.0)
                out_ref[w] = acc

        @pl.when(is_far)
        def _():
            for buffer, sem in ((straight_ids, straight_id_send), (straight, straight_send)):
                sent = buffer.at[0, pl.ds(0, len(firsts))]
                pltpu.make_async_copy(sent, sent, sem).wait()

    pltpu.make_async_copy(recv_last, recv_last, xl_send).wait()
    pltpu.make_async_copy(recv_rest, recv_rest, xr_send).wait()
    pltpu.make_async_copy(ids.at[others], ids.at[others], id_send).wait()
    pltpu.make_async_copy(held.at[others], held.at[others], held_send).wait()
    for s in range(3):
        pltpu.make_async_copy(fixed_out.at[s], fixed_out.at[s], fixed_send.at[s]).wait()
    pltpu.make_async_copy(landed, landed, y_send).wait()


def local(ny, nz, nx, tokens, out_grad, proj_in, proj_out, source_ids, slot_of_source):
    length = tokens.shape[0] // source_ids.shape[0]
    pin, pout = proj_in.T, proj_out.T
    spread = ny * CORES
    dma, regular = pltpu.SemaphoreType.DMA, pltpu.SemaphoreType.REGULAR
    out = pl.pallas_call(
        functools.partial(kernel, ny, nz, nx, length),
        out_shape=pltpu.VMEM((2, 8, 128), F32),
        in_specs=[pl.BlockSpec(memory_space=pl.ANY)] * 6,
        out_specs=pl.BlockSpec(memory_space=pltpu.VMEM),
        scratch_shapes=[
            pltpu.VMEM(tokens.shape, tokens.dtype),
            pltpu.VMEM(out_grad.shape, out_grad.dtype),
            pltpu.VMEM(pin.shape, pin.dtype),
            pltpu.VMEM(pout.shape, pout.dtype),
            pltpu.SMEM(source_ids.shape, jnp.int32),
            pltpu.SMEM(slot_of_source.shape, jnp.int32),
            pltpu.VMEM((4, 64, length), F32),
            pltpu.VMEM((nx, PACKED, 128), F32),
            pltpu.VMEM((nx, 3, PACKED, 128), F32),
            pltpu.VMEM((nx - 1, PACKED, 128), F32),
            pltpu.VMEM((nx - 1, 3, PACKED, 128), F32),
            pltpu.VMEM((nz, 8, 128), F32),
            pltpu.VMEM((nz, 1, 128), jnp.int32),
            pltpu.VMEM((3, 2, 8, 128), F32),
            pltpu.VMEM((3, 2, 8, 128), F32),
            pltpu.VMEM((spread, 2, 8, 128), F32),
            pltpu.VMEM((spread, 2, 8, 128), F32),
            pltpu.VMEM((FAR, spread, 8, 128), F32),
            pltpu.VMEM((FAR, spread, 1, 128), jnp.int32),
            dma, dma, dma, dma,
            dma((8,)), dma, dma, dma, dma, dma, dma, dma, dma((2,)), dma((3,)), dma((3,)), dma, dma,
            regular, regular,
        ],
        compiler_params=pltpu.CompilerParams(
            collective_id=0, has_side_effects=True, vmem_limit_bytes=60 * 2**20
        ),
    )(tokens, out_grad, pin, pout, source_ids, slot_of_source)
    return out.reshape(2, 8 * 128)


def solution(mesh):
    nx, ndp = mesh.shape["tensor"], mesh.shape["dp"]
    ny = COLUMNS
    nz = ndp // (ny * CORES)
    placed = (
        P("dp", "tensor"),
        P("dp", "tensor"),
        P("tensor", None),
        P("tensor", None),
        P("dp"),
        P(),
    )
    return jax.shard_map(
        functools.partial(local, ny, nz, nx),
        mesh=mesh, in_specs=placed, out_specs=P("dp", "tensor"), check_vma=False,
    )
```

```python
import functools

import jax
import jax.numpy as jnp
from jax import lax
from jax.experimental import pallas as pl
from jax.experimental.pallas import tpu as pltpu
from jax.sharding import PartitionSpec as P

MESH = pl.DeviceIdType.MESH
F32 = jnp.float32
CORES = 2
COLUMNS = 4
HEADS = 4
FIRST = ((0, 1),)
FAR = 7
PACKED = 40


def away(d, n):
    return min(d, n - d)


def product(a, b):
    return lax.dot_general(a, b, (((1,), (1,)), ((), ())), preferred_element_type=F32)


def kernel(
    ny, nz, nx, length,
    tok_hbm, og_hbm, pin_hbm, pout_hbm, src_hbm, slot_hbm,
    out_ref,
    tok, og, pin, pout, src, slot_of, gpt,
    mine_last, mine_rest, recv_last, recv_rest,
    held, ids, fixed_out, fixed_in, y_out, y_in,
    straight, straight_ids, straight_send, straight_recv, straight_id_send, straight_id_recv,
    load_sem, xl_send, xl_recv, xr_send, xr_recv,
    id_send, id_recv, held_send, held_recv,
    fixed_send, fixed_recv, y_send, y_recv, token_a, token_b,
):
    j = lax.axis_index("dp")
    m = lax.axis_index("tensor")
    ndp = ny * nz * CORES
    half = ndp // 2
    core = lax.rem(j, CORES)
    z = lax.rem(lax.div(j, CORES), nz)
    y = lax.div(j, CORES * nz)

    def dp_of(yy, zz, cc):
        return (yy * nz + zz) * CORES + cc

    def rows_of(s):
        return pl.ds(s * length, length)

    last, rest = rows_of(3), pl.ds(0, 3 * length)
    loads = [
        (pout_hbm, pout),
        (og_hbm.at[last], og.at[last]),
        (pin_hbm, pin),
        (tok_hbm.at[last], tok.at[last]),
        (src_hbm, src),
        (slot_hbm, slot_of),
        (og_hbm.at[rest], og.at[rest]),
        (tok_hbm.at[rest], tok.at[rest]),
    ]
    loads = [pltpu.make_async_copy(a, b, load_sem.at[i]) for i, (a, b) in enumerate(loads)]
    for load in loads:
        load.start()

    def z_peers(offsets):
        offsets = sorted({d % nz for d in offsets} - {0})
        return [(dp_of(y, lax.rem(z + d, nz), core), m) for d in offsets]

    def greet(sem, peers):
        for peer in peers:
            pl.semaphore_signal(sem, inc=1, device_id=peer, device_id_type=MESH)

    x_peers = [(j, lax.rem(m + d, nx)) for d in range(1, nx)]
    spread = [(dy, dc) for dy in range(ny) for dc in range(CORES)]
    spread_peers = [
        (dp_of(lax.rem(y + dy, ny), z, lax.rem(core + dc, CORES)), m) for dy, dc in spread
    ]
    x_order = sorted(range(1, nx), key=lambda d: -away(d, nx))
    spread_order = sorted(
        range(1, len(spread)), key=lambda t: (-away(spread[t][0], ny), -spread[t][1])
    )
    fixed_to = [lax.rem(j + ndp - 1, ndp), lax.rem(j + 1, ndp), lax.rem(j + half, ndp)]
    beside = lax.rem(j + ndp + 2 * core - 1, ndp)
    near = x_peers + spread_peers[1:] + z_peers((1, 2, -1, -2)) + [(beside, m)]
    two_off, four_off = z_peers((2, -2)), z_peers((4, -4))
    barrier = pltpu.get_barrier_semaphore()
    greet(barrier, near)
    heads = HEADS if nz >= 16 else 0

    @pl.when(z < heads)
    def _():
        greet(barrier, z_peers(range(1, nz)))

    begin, end = nz // 2 - FAR // 2 + 1, nz // 2 + FAR // 2 + 2
    far = range(begin, end) if heads else range(0)
    firsts = FIRST if heads else ()
    is_far = jnp.logical_and(z >= begin, z < end)
    far_group = lax.div(z + nz - begin, nz) - lax.div(z + nz - end, nz)

    def at_first(yy, cc):
        at = z < 0
        for fy, fc in firsts:
            at = jnp.logical_or(at, jnp.logical_and(yy == fy, cc == fc))
        return at

    is_first = jnp.logical_and(z == 0, at_first(y, core))

    @pl.when(is_first)
    def _():
        for zz in far:
            greet(barrier, [(dp_of(yy, zz, cc), m) for yy in range(ny) for cc in range(CORES)])


    def project(s, store):
        rows = rows_of(s)
        xp = product(tok[rows, :], pin[...])
        xp = jnp.concatenate([xp[: length // 2], xp[length // 2 :]], axis=1)
        gpt[s, 0:64, :] = product(pout[...], og[rows, :])
        for q in range(nx):
            even = gpt[s, pl.ds(16 * q, 8, stride=2), :]
            odd = gpt[s, pl.ds(16 * q + 1, 8, stride=2), :]
            store(q, xp, jnp.concatenate([even, odd], axis=1))

    def store_last(q, xp, gq):
        mine_last[q, 0:32, :] = xp
        mine_last[q, 32:40, :] = gq

    for i in range(4):
        loads[i].wait()
    project(3, store_last)

    @pl.when(z < heads)
    def _():
        pl.semaphore_wait(barrier, len(near) + heads - 1)

    @pl.when(jnp.logical_and(z >= heads, jnp.logical_not(is_far)))
    def _():
        pl.semaphore_wait(barrier, len(near) + heads)

    if heads:
        @pl.when(is_far)
        def _():
            pl.semaphore_wait(barrier, len(near) + heads + len(firsts))

    for d in x_order:
        pltpu.make_async_remote_copy(
            mine_last.at[x_peers[d - 1][1]], recv_last.at[nx - 1 - d], xl_send, xl_recv,
            device_id=x_peers[d - 1], device_id_type=MESH,
        ).start()
    greet(token_a, two_off)

    loads[4].wait()
    loads[5].wait()
    slots = [slot_of[src[i]] for i in range(4)]
    ids[0] = jnp.full((1, 128), slots[3], jnp.int32)

    def along_z(source, targets, send_sem, recv_sem):
        for zz in targets:
            @pl.when(z != zz)
            def _():
                pltpu.make_async_remote_copy(
                    source.at[0], source.at[lax.rem(z - zz + nz, nz)], send_sem, recv_sem,
                    device_id=(dp_of(y, zz, core), m), device_id_type=MESH,
                ).start()

    def to_first(source, target, send_sem, recv_sem):
        if not firsts:
            return

        @pl.when(is_far)
        def _():
            for fy, fc in firsts:
                pltpu.make_async_remote_copy(
                    source.at[0], target.at[z - far[0], y * CORES + core], send_sem, recv_sem,
                    device_id=(dp_of(fy, 0, fc), m), device_id_type=MESH,
                ).start()

    early, late = range(heads), range(heads, nz)
    to_first(ids, straight_ids, straight_id_send, straight_id_recv)
    along_z(ids, early, id_send, id_recv)

    pl.semaphore_wait(token_a, len(two_off))
    greet(token_b, four_off)

    loads[6].wait()
    loads[7].wait()
    for s in range(3):
        def store_rest(q, xp, gq):
            mine_rest[q, s, 0:32, :] = xp
            mine_rest[q, s, 32:40, :] = gq

        project(s, store_rest)

    low = lax.broadcasted_iota(jnp.int32, (32, 128), 1) < 64

    def sketch(total):
        xp, gq = total[0:32], total[32:40]
        turned = pltpu.roll(xp, 64, 1)
        twice = jnp.concatenate(
            [
                jnp.where(low, xp, 0.0), jnp.where(low, turned, 0.0),
                jnp.where(low, 0.0, turned), jnp.where(low, 0.0, xp),
            ],
            axis=0,
        )
        value = lax.dot_general(
            gq, twice, (((1,), (0,)), ((), ())),
            precision=lax.Precision.HIGHEST, preferred_element_type=F32,
        )
        return value * (length ** -0.5)

    pltpu.make_async_copy(recv_last, recv_last, xl_recv).wait()
    total = mine_last[m]
    for d in range(nx - 1):
        total = total + recv_last[d]
    held[0] = sketch(total)
    along_z(held, range(1), held_send, held_recv.at[far_group])
    to_first(held, straight, straight_send, straight_recv)
    along_z(held, range(1, heads), held_send, held_recv.at[far_group])
    for d in x_order:
        pltpu.make_async_remote_copy(
            mine_rest.at[x_peers[d - 1][1]], recv_rest.at[nx - 1 - d], xr_send, xr_recv,
            device_id=x_peers[d - 1], device_id_type=MESH,
        ).start()

    if four_off:
        pl.semaphore_wait(token_b, len(four_off))
    along_z(ids, late, id_send, id_recv)
    along_z(held, late, held_send, held_recv.at[far_group])

    pltpu.make_async_copy(recv_rest, recv_rest, xr_recv).wait()
    for s in range(3):
        total = mine_rest[m, s]
        for d in range(nx - 1):
            total = total + recv_rest[d, s]
        value = sketch(total)
        for w in range(2):
            weight = jnp.where(slots[s] == fixed_to[s] * 2 + w, 1.0, 0.0).astype(F32)
            fixed_out[s, w] = value * weight
        pltpu.make_async_remote_copy(
            fixed_out.at[s], fixed_in.at[s], fixed_send.at[s], fixed_recv.at[s],
            device_id=(fixed_to[s], m), device_id_type=MESH,
        ).start()

    others = pl.ds(1, nz - 1)
    pltpu.make_async_copy(ids.at[others], ids.at[others], id_recv).wait()

    def arrived(count, group):
        slots = held.at[pl.ds(0, count)]
        pltpu.make_async_copy(slots, slots, held_recv.at[group]).wait()

    def add(t, slots, fresh):
        base = spread_peers[t][0] * 2
        for w in range(2):
            acc = jnp.zeros((8, 128), F32) if fresh else y_out[t, w]
            for i in slots:
                acc = acc + jnp.where(ids[i] == base + w, held[i], 0.0)
            y_out[t, w] = acc

    def to_spread(t):
        if t:
            dy, dc = spread[t]
            back = ((ny - dy) % ny) * CORES + dc
            pltpu.make_async_remote_copy(
                y_out.at[t], y_in.at[back], y_send, y_recv,
                device_id=spread_peers[t], device_id_type=MESH,
            ).start()

    def goes_first(t):
        dy, dc = spread[t]
        return at_first(lax.rem(y + dy, ny), lax.rem(core + dc, CORES))

    if heads:
        @pl.when(z == 0)
        def _():
            arrived(nz - 1 - len(far), 0)
            for t in spread_order + [0]:
                add(t, [i for i in range(nz) if i not in far], True)

                @pl.when(goes_first(t))
                def _():
                    to_spread(t)

            arrived(len(far), 1)
            for t in spread_order + [0]:
                @pl.when(jnp.logical_not(goes_first(t)))
                def _():
                    add(t, far, False)
                    to_spread(t)

    @pl.when(z >= (1 if heads else 0))
    def _():
        if heads:
            @pl.when(is_far)
            def _():
                arrived(nz - len(far), 0)
                arrived(len(far) - 1, 1)

            @pl.when(jnp.logical_not(is_far))
            def _():
                arrived(nz - 1 - len(far), 0)
                arrived(len(far), 1)
        else:
            arrived(nz - 1, 0)
        for t in spread_order + [0]:
            add(t, range(nz), True)
            to_spread(t)

    for s in range(3):
        pltpu.make_async_copy(fixed_in.at[s], fixed_in.at[s], fixed_recv.at[s]).wait()
    landed = y_in.at[pl.ds(1, len(spread) - 1)]
    pltpu.make_async_copy(landed, landed, y_recv).wait()
    for w in range(2):
        acc = y_out[0, w]
        for s in range(3):
            acc = acc + fixed_in[s, w]
        for t in range(1, len(spread)):
            acc = acc + y_in[t, w]
        out_ref[w] = acc

    if firsts:
        @pl.when(is_first)
        def _():
            for buffer, sem in ((straight_ids, straight_id_recv), (straight, straight_recv)):
                pltpu.make_async_copy(buffer, buffer, sem).wait()
            for w in range(2):
                acc = out_ref[w]
                for i in range(len(far)):
                    for t in range(len(spread)):
                        acc = acc + jnp.where(straight_ids[i, t] == j * 2 + w, straight[i, t], 0.0)
                out_ref[w] = acc

        @pl.when(is_far)
        def _():
            for buffer, sem in ((straight_ids, straight_id_send), (straight, straight_send)):
                sent = buffer.at[0, pl.ds(0, len(firsts))]
                pltpu.make_async_copy(sent, sent, sem).wait()

    pltpu.make_async_copy(recv_last, recv_last, xl_send).wait()
    pltpu.make_async_copy(recv_rest, recv_rest, xr_send).wait()
    pltpu.make_async_copy(ids.at[others], ids.at[others], id_send).wait()
    pltpu.make_async_copy(held.at[others], held.at[others], held_send).wait()
    for s in range(3):
        pltpu.make_async_copy(fixed_out.at[s], fixed_out.at[s], fixed_send.at[s]).wait()
    pltpu.make_async_copy(landed, landed, y_send).wait()


def local(ny, nz, nx, tokens, out_grad, proj_in, proj_out, source_ids, slot_of_source):
    length = tokens.shape[0] // source_ids.shape[0]
    pin, pout = proj_in.T, proj_out.T
    spread = ny * CORES
    dma, regular = pltpu.SemaphoreType.DMA, pltpu.SemaphoreType.REGULAR
    out = pl.pallas_call(
        functools.partial(kernel, ny, nz, nx, length),
        out_shape=pltpu.VMEM((2, 8, 128), F32),
        in_specs=[pl.BlockSpec(memory_space=pl.ANY)] * 6,
        out_specs=pl.BlockSpec(memory_space=pltpu.VMEM),
        scratch_shapes=[
            pltpu.VMEM(tokens.shape, tokens.dtype),
            pltpu.VMEM(out_grad.shape, out_grad.dtype),
            pltpu.VMEM(pin.shape, pin.dtype),
            pltpu.VMEM(pout.shape, pout.dtype),
            pltpu.SMEM(source_ids.shape, jnp.int32),
            pltpu.SMEM(slot_of_source.shape, jnp.int32),
            pltpu.VMEM((4, 72, length), F32),
            pltpu.VMEM((nx, PACKED, 128), F32),
            pltpu.VMEM((nx, 3, PACKED, 128), F32),
            pltpu.VMEM((nx - 1, PACKED, 128), F32),
            pltpu.VMEM((nx - 1, 3, PACKED, 128), F32),
            pltpu.VMEM((nz, 8, 128), F32),
            pltpu.VMEM((nz, 1, 128), jnp.int32),
            pltpu.VMEM((3, 2, 8, 128), F32),
            pltpu.VMEM((3, 2, 8, 128), F32),
            pltpu.VMEM((spread, 2, 8, 128), F32),
            pltpu.VMEM((spread, 2, 8, 128), F32),
            pltpu.VMEM((FAR, spread, 8, 128), F32),
            pltpu.VMEM((FAR, spread, 1, 128), jnp.int32),
            dma, dma, dma, dma,
            dma((8,)), dma, dma, dma, dma, dma, dma, dma, dma((2,)), dma((3,)), dma((3,)), dma, dma,
            regular, regular,
        ],
        compiler_params=pltpu.CompilerParams(
            collective_id=0, has_side_effects=True, vmem_limit_bytes=60 * 2**20
        ),
    )(tokens, out_grad, pin, pout, source_ids, slot_of_source)
    return out.reshape(2, 8 * 128)


def solution(mesh):
    nx, ndp = mesh.shape["tensor"], mesh.shape["dp"]
    ny = COLUMNS
    nz = ndp // (ny * CORES)
    placed = (
        P("dp", "tensor"),
        P("dp", "tensor"),
        P("tensor", None),
        P("tensor", None),
        P("dp"),
        P(),
    )
    return jax.shard_map(
        functools.partial(local, ny, nz, nx),
        mesh=mesh, in_specs=placed, out_specs=P("dp", "tensor"), check_vma=False,
    )
```

```python
import functools

import jax
import jax.numpy as jnp
from jax import lax
from jax.experimental import pallas as pl
from jax.experimental.pallas import tpu as pltpu
from jax.sharding import PartitionSpec as P

MESH = pl.DeviceIdType.MESH
F32 = jnp.float32
CORES = 2
COLUMNS = 4
HEADS = 4
FIRST = ((0, 1), (1, 1))
FAR = 7
PACKED = 40


def away(d, n):
    return min(d, n - d)


def product(a, b):
    return lax.dot_general(a, b, (((1,), (1,)), ((), ())), preferred_element_type=F32)


def kernel(
    ny, nz, nx, length,
    tok_hbm, og_hbm, pin_hbm, pout_hbm, src_hbm, slot_hbm,
    out_ref,
    tok, og, pin, pout, src, slot_of, gpt,
    mine_last, mine_rest, recv_last, recv_rest,
    held, ids, fixed_out, fixed_in, y_out, y_in,
    straight, straight_ids, straight_send, straight_recv, straight_id_send, straight_id_recv,
    load_sem, xl_send, xl_recv, xr_send, xr_recv,
    id_send, id_recv, held_send, held_recv,
    fixed_send, fixed_recv, y_send, y_recv, token_a, token_b,
):
    j = lax.axis_index("dp")
    m = lax.axis_index("tensor")
    ndp = ny * nz * CORES
    half = ndp // 2
    core = lax.rem(j, CORES)
    z = lax.rem(lax.div(j, CORES), nz)
    y = lax.div(j, CORES * nz)

    def dp_of(yy, zz, cc):
        return (yy * nz + zz) * CORES + cc

    def rows_of(s):
        return pl.ds(s * length, length)

    last, rest = rows_of(3), pl.ds(0, 3 * length)
    loads = [
        (pout_hbm, pout),
        (og_hbm.at[last], og.at[last]),
        (pin_hbm, pin),
        (tok_hbm.at[last], tok.at[last]),
        (src_hbm, src),
        (slot_hbm, slot_of),
        (og_hbm.at[rest], og.at[rest]),
        (tok_hbm.at[rest], tok.at[rest]),
    ]
    loads = [pltpu.make_async_copy(a, b, load_sem.at[i]) for i, (a, b) in enumerate(loads)]
    for load in loads:
        load.start()

    def z_peers(offsets):
        offsets = sorted({d % nz for d in offsets} - {0})
        return [(dp_of(y, lax.rem(z + d, nz), core), m) for d in offsets]

    def greet(sem, peers):
        for peer in peers:
            pl.semaphore_signal(sem, inc=1, device_id=peer, device_id_type=MESH)

    x_peers = [(j, lax.rem(m + d, nx)) for d in range(1, nx)]
    spread = [(dy, dc) for dy in range(ny) for dc in range(CORES)]
    spread_peers = [
        (dp_of(lax.rem(y + dy, ny), z, lax.rem(core + dc, CORES)), m) for dy, dc in spread
    ]
    x_order = sorted(range(1, nx), key=lambda d: -away(d, nx))
    spread_order = sorted(
        range(1, len(spread)), key=lambda t: (-away(spread[t][0], ny), -spread[t][1])
    )
    fixed_to = [lax.rem(j + ndp - 1, ndp), lax.rem(j + 1, ndp), lax.rem(j + half, ndp)]
    beside = lax.rem(j + ndp + 2 * core - 1, ndp)
    near = x_peers + spread_peers[1:] + z_peers((1, 2, -1, -2)) + [(beside, m)]
    two_off, four_off = z_peers((2, -2)), z_peers((4, -4))
    barrier = pltpu.get_barrier_semaphore()
    greet(barrier, near)
    heads = HEADS if nz >= 16 else 0

    @pl.when(z < heads)
    def _():
        greet(barrier, z_peers(range(1, nz)))

    begin, end = nz // 2 - FAR // 2 + 1, nz // 2 + FAR // 2 + 2
    far = range(begin, end) if heads else range(0)
    firsts = FIRST if heads else ()
    is_far = jnp.logical_and(z >= begin, z < end)
    far_group = lax.div(z + nz - begin, nz) - lax.div(z + nz - end, nz)

    def at_first(yy, cc):
        at = z < 0
        for fy, fc in firsts:
            at = jnp.logical_or(at, jnp.logical_and(yy == fy, cc == fc))
        return at

    is_first = jnp.logical_and(z == 0, at_first(y, core))

    @pl.when(is_first)
    def _():
        for zz in far:
            greet(barrier, [(dp_of(yy, zz, cc), m) for yy in range(ny) for cc in range(CORES)])


    def project(s, store):
        rows = rows_of(s)
        xp = product(tok[rows, :], pin[...])
        xp = jnp.concatenate([xp[: length // 2], xp[length // 2 :]], axis=1)
        gpt[s, 0:64, :] = product(pout[...], og[rows, :])
        for q in range(nx):
            even = gpt[s, pl.ds(16 * q, 8, stride=2), :]
            odd = gpt[s, pl.ds(16 * q + 1, 8, stride=2), :]
            store(q, xp, jnp.concatenate([even, odd], axis=1))

    def store_last(q, xp, gq):
        mine_last[q, 0:32, :] = xp
        mine_last[q, 32:40, :] = gq

    for i in range(4):
        loads[i].wait()
    project(3, store_last)

    @pl.when(z < heads)
    def _():
        pl.semaphore_wait(barrier, len(near) + heads - 1)

    @pl.when(jnp.logical_and(z >= heads, jnp.logical_not(is_far)))
    def _():
        pl.semaphore_wait(barrier, len(near) + heads)

    if heads:
        @pl.when(is_far)
        def _():
            pl.semaphore_wait(barrier, len(near) + heads + len(firsts))

    for d in x_order:
        pltpu.make_async_remote_copy(
            mine_last.at[x_peers[d - 1][1]], recv_last.at[nx - 1 - d], xl_send, xl_recv,
            device_id=x_peers[d - 1], device_id_type=MESH,
        ).start()
    greet(token_a, two_off)

    loads[4].wait()
    loads[5].wait()
    slots = [slot_of[src[i]] for i in range(4)]
    ids[0] = jnp.full((1, 128), slots[3], jnp.int32)

    def along_z(source, targets, send_sem, recv_sem):
        for zz in targets:
            @pl.when(z != zz)
            def _():
                pltpu.make_async_remote_copy(
                    source.at[0], source.at[lax.rem(z - zz + nz, nz)], send_sem, recv_sem,
                    device_id=(dp_of(y, zz, core), m), device_id_type=MESH,
                ).start()

    def to_first(source, target, send_sem, recv_sem):
        if not firsts:
            return

        @pl.when(is_far)
        def _():
            for fy, fc in firsts:
                pltpu.make_async_remote_copy(
                    source.at[0], target.at[z - far[0], y * CORES + core], send_sem, recv_sem,
                    device_id=(dp_of(fy, 0, fc), m), device_id_type=MESH,
                ).start()

    early, late = range(heads), range(heads, nz)
    to_first(ids, straight_ids, straight_id_send, straight_id_recv)
    along_z(ids, early, id_send, id_recv)

    pl.semaphore_wait(token_a, len(two_off))
    greet(token_b, four_off)

    loads[6].wait()
    loads[7].wait()
    for s in range(3):
        def store_rest(q, xp, gq):
            mine_rest[q, s, 0:32, :] = xp
            mine_rest[q, s, 32:40, :] = gq

        project(s, store_rest)

    low = lax.broadcasted_iota(jnp.int32, (32, 128), 1) < 64

    def sketch(total):
        xp, gq = total[0:32], total[32:40]
        turned = pltpu.roll(xp, 64, 1)
        twice = jnp.concatenate(
            [
                jnp.where(low, xp, 0.0), jnp.where(low, turned, 0.0),
                jnp.where(low, 0.0, turned), jnp.where(low, 0.0, xp),
            ],
            axis=0,
        )
        value = lax.dot_general(
            gq, twice, (((1,), (0,)), ((), ())),
            precision=lax.Precision.HIGHEST, preferred_element_type=F32,
        )
        return value * (length ** -0.5)

    pltpu.make_async_copy(recv_last, recv_last, xl_recv).wait()
    total = mine_last[m]
    for d in range(nx - 1):
        total = total + recv_last[d]
    held[0] = sketch(total)
    along_z(held, range(1), held_send, held_recv.at[far_group])
    to_first(held, straight, straight_send, straight_recv)
    along_z(held, range(1, heads), held_send, held_recv.at[far_group])
    for d in x_order:
        pltpu.make_async_remote_copy(
            mine_rest.at[x_peers[d - 1][1]], recv_rest.at[nx - 1 - d], xr_send, xr_recv,
            device_id=x_peers[d - 1], device_id_type=MESH,
        ).start()

    if four_off:
        pl.semaphore_wait(token_b, len(four_off))
    along_z(ids, late, id_send, id_recv)
    along_z(held, late, held_send, held_recv.at[far_group])

    pltpu.make_async_copy(recv_rest, recv_rest, xr_recv).wait()
    for s in range(3):
        total = mine_rest[m, s]
        for d in range(nx - 1):
            total = total + recv_rest[d, s]
        value = sketch(total)
        for w in range(2):
            weight = jnp.where(slots[s] == fixed_to[s] * 2 + w, 1.0, 0.0).astype(F32)
            fixed_out[s, w] = value * weight
        pltpu.make_async_remote_copy(
            fixed_out.at[s], fixed_in.at[s], fixed_send.at[s], fixed_recv.at[s],
            device_id=(fixed_to[s], m), device_id_type=MESH,
        ).start()

    others = pl.ds(1, nz - 1)
    pltpu.make_async_copy(ids.at[others], ids.at[others], id_recv).wait()

    def arrived(count, group):
        slots = held.at[pl.ds(0, count)]
        pltpu.make_async_copy(slots, slots, held_recv.at[group]).wait()

    def add(t, slots, fresh):
        base = spread_peers[t][0] * 2
        for w in range(2):
            acc = jnp.zeros((8, 128), F32) if fresh else y_out[t, w]
            for i in slots:
                acc = acc + jnp.where(ids[i] == base + w, held[i], 0.0)
            y_out[t, w] = acc

    def to_spread(t):
        if t:
            dy, dc = spread[t]
            back = ((ny - dy) % ny) * CORES + dc
            pltpu.make_async_remote_copy(
                y_out.at[t], y_in.at[back], y_send, y_recv,
                device_id=spread_peers[t], device_id_type=MESH,
            ).start()

    def goes_first(t):
        dy, dc = spread[t]
        return at_first(lax.rem(y + dy, ny), lax.rem(core + dc, CORES))

    if heads:
        @pl.when(z == 0)
        def _():
            arrived(nz - 1 - len(far), 0)
            for t in spread_order + [0]:
                add(t, [i for i in range(nz) if i not in far], True)

                @pl.when(goes_first(t))
                def _():
                    to_spread(t)

            arrived(len(far), 1)
            for t in spread_order + [0]:
                @pl.when(jnp.logical_not(goes_first(t)))
                def _():
                    add(t, far, False)
                    to_spread(t)

    @pl.when(z >= (1 if heads else 0))
    def _():
        if heads:
            @pl.when(is_far)
            def _():
                arrived(nz - len(far), 0)
                arrived(len(far) - 1, 1)

            @pl.when(jnp.logical_not(is_far))
            def _():
                arrived(nz - 1 - len(far), 0)
                arrived(len(far), 1)
        else:
            arrived(nz - 1, 0)
        for t in spread_order + [0]:
            add(t, range(nz), True)
            to_spread(t)

    for s in range(3):
        pltpu.make_async_copy(fixed_in.at[s], fixed_in.at[s], fixed_recv.at[s]).wait()
    landed = y_in.at[pl.ds(1, len(spread) - 1)]
    pltpu.make_async_copy(landed, landed, y_recv).wait()
    for w in range(2):
        acc = y_out[0, w]
        for s in range(3):
            acc = acc + fixed_in[s, w]
        for t in range(1, len(spread)):
            acc = acc + y_in[t, w]
        out_ref[w] = acc

    if firsts:
        @pl.when(is_first)
        def _():
            for buffer, sem in ((straight_ids, straight_id_recv), (straight, straight_recv)):
                pltpu.make_async_copy(buffer, buffer, sem).wait()
            for w in range(2):
                acc = out_ref[w]
                for i in range(len(far)):
                    for t in range(len(spread)):
                        acc = acc + jnp.where(straight_ids[i, t] == j * 2 + w, straight[i, t], 0.0)
                out_ref[w] = acc

        @pl.when(is_far)
        def _():
            for buffer, sem in ((straight_ids, straight_id_send), (straight, straight_send)):
                sent = buffer.at[0, pl.ds(0, len(firsts))]
                pltpu.make_async_copy(sent, sent, sem).wait()

    pltpu.make_async_copy(recv_last, recv_last, xl_send).wait()
    pltpu.make_async_copy(recv_rest, recv_rest, xr_send).wait()
    pltpu.make_async_copy(ids.at[others], ids.at[others], id_send).wait()
    pltpu.make_async_copy(held.at[others], held.at[others], held_send).wait()
    for s in range(3):
        pltpu.make_async_copy(fixed_out.at[s], fixed_out.at[s], fixed_send.at[s]).wait()
    pltpu.make_async_copy(landed, landed, y_send).wait()


def local(ny, nz, nx, tokens, out_grad, proj_in, proj_out, source_ids, slot_of_source):
    length = tokens.shape[0] // source_ids.shape[0]
    pin, pout = proj_in.T, proj_out.T
    spread = ny * CORES
    dma, regular = pltpu.SemaphoreType.DMA, pltpu.SemaphoreType.REGULAR
    out = pl.pallas_call(
        functools.partial(kernel, ny, nz, nx, length),
        out_shape=pltpu.VMEM((2, 8, 128), F32),
        in_specs=[pl.BlockSpec(memory_space=pl.ANY)] * 6,
        out_specs=pl.BlockSpec(memory_space=pltpu.VMEM),
        scratch_shapes=[
            pltpu.VMEM(tokens.shape, tokens.dtype),
            pltpu.VMEM(out_grad.shape, out_grad.dtype),
            pltpu.VMEM(pin.shape, pin.dtype),
            pltpu.VMEM(pout.shape, pout.dtype),
            pltpu.SMEM(source_ids.shape, jnp.int32),
            pltpu.SMEM(slot_of_source.shape, jnp.int32),
            pltpu.VMEM((4, 72, length), F32),
            pltpu.VMEM((nx, PACKED, 128), F32),
            pltpu.VMEM((nx, 3, PACKED, 128), F32),
            pltpu.VMEM((nx - 1, PACKED, 128), F32),
            pltpu.VMEM((nx - 1, 3, PACKED, 128), F32),
            pltpu.VMEM((nz, 8, 128), F32),
            pltpu.VMEM((nz, 1, 128), jnp.int32),
            pltpu.VMEM((3, 2, 8, 128), F32),
            pltpu.VMEM((3, 2, 8, 128), F32),
            pltpu.VMEM((spread, 2, 8, 128), F32),
            pltpu.VMEM((spread, 2, 8, 128), F32),
            pltpu.VMEM((FAR, spread, 8, 128), F32),
            pltpu.VMEM((FAR, spread, 1, 128), jnp.int32),
            dma, dma, dma, dma,
            dma((8,)), dma, dma, dma, dma, dma, dma, dma, dma((2,)), dma((3,)), dma((3,)), dma, dma,
            regular, regular,
        ],
        compiler_params=pltpu.CompilerParams(
            collective_id=0, has_side_effects=True, vmem_limit_bytes=60 * 2**20
        ),
    )(tokens, out_grad, pin, pout, source_ids, slot_of_source)
    return out.reshape(2, 8 * 128)


def solution(mesh):
    nx, ndp = mesh.shape["tensor"], mesh.shape["dp"]
    ny = COLUMNS
    nz = ndp // (ny * CORES)
    placed = (
        P("dp", "tensor"),
        P("dp", "tensor"),
        P("tensor", None),
        P("tensor", None),
        P("dp"),
        P(),
    )
    return jax.shard_map(
        functools.partial(local, ny, nz, nx),
        mesh=mesh, in_specs=placed, out_specs=P("dp", "tensor"), check_vma=False,
    )
```
